32 devices in a mesh: groups: 2 (over y), chol: 4 (over z), walk: 2 (over x), orb: 2 (over core).
Axes of the slice: x: 2, y: 2, z: 4, core: 2. Of those that a mesh axis runs over, the one named last changes fastest.
Arguments:
- walkers: float32 [32, 2, 36864], P(('groups', 'walk'), None, ('chol', 'orb')), parts along dimension 0, may hold values from -6 to 6
- correlation_inverse: float32 [32, 2, 96, 96], P(('groups', 'walk')), parts along dimension 0, may hold values from -0.625 to 0.625
- half_vectors: bfloat16 [4096, 36864], P(('groups', 'walk'), ('chol', 'orb')), parts along dimension 0, may hold values from -0.01953125 to 0.01953125
- field_vectors: bfloat16 [4096, 384, 384], P(('groups', 'walk'), ('chol', 'orb')), parts along dimension 0, may hold values from -0.0048828125 to 0.0048828125
- samples: float32 [32, 2048], P('groups', 'walk'), parts along dimension 0, may hold values from -6 to 6
- source: int32 [32], P(('groups', 'walk')), parts along dimension 0, may hold values from 0 to 15
Outputs:
- walkers_next: float32 [32, 2, 36864], P(('groups', 'walk'), None, ('chol', 'orb')), parts along dimension 0
The draws below stay inside these ranges and needn't reach their ends.
There are 2 independent parts, one for each index of `groups`. The reference program is written for one: setup_inputs(seed, part) draws one part's arguments, and reference() takes and returns one part's arrays. A program takes and returns all parts, laid end to end along the dimension named above; each array names one. Nothing has to cross between parts.
All inputs are finite; a program needn't handle non-finite values.
Results may differ from the reference program's by a relative error of at most 0.02.
Values may be sent and summed in bfloat16 or wider, within the bound.
A program may use at most 128 MiB of HBM per device.

```python
import math
import jax
import jax.numpy as jnp
import numpy as np
from jax import lax

M = 384
N = 96
G = 2048
TERMS = 4
NS_STEPS = 2
W = 16


def touch_ends(array, key, least, largest):
    index_at = [jax.random.randint(jax.random.fold_in(key, axis), (), 0, length) for axis, length in enumerate(array.shape)]
    main_axis = array.shape.index(max(array.shape))
    beside = index_at[:main_axis] + [(index_at[main_axis] + 1) % array.shape[main_axis]] + index_at[main_axis + 1:]
    return array.at[tuple(index_at)].set(least).at[tuple(beside)].set(largest)


def shard_levels(key, shape, shards, smallest, top_value):
    def one(dim, parts):
        draws = jax.random.uniform(jax.random.fold_in(jax.random.fold_in(key, 6), dim), (parts,), jnp.float32, smallest / len(shards), top_value / len(shards))
        return jnp.repeat(jnp.exp(draws), shape[dim] // parts).reshape((-1,) + (1,) * (len(shape) - dim - 1))

    factor_of = one(*shards[0])
    for cut in shards[1:]:
        factor_of = factor_of * one(*cut)
    return factor_of


def rank_table(amount, skew):
    loads = [(1 << 20) // math.isqrt(rank ** skew) + 1 for rank in range(1, amount + 1)]
    spread = 1 + sum(loads) // (1 << 30)
    return np.cumsum(np.array([max(1, weight // spread) for weight in loads]))


def ranked(key, dims, amount, skew):
    table = rank_table(amount, skew)
    pick = jax.random.randint(jax.random.fold_in(key, 1), dims, 0, int(table[amount - 1]))
    rank = jnp.searchsorted(jnp.asarray(table, jnp.int32), pick, side="right")
    return jax.random.permutation(jax.random.fold_in(key, 2), amount)[rank].astype(jnp.int32)


def bell_draw(stream_key, shape, scale, limit, shards=(), kind=jnp.bfloat16):
    drawn = jax.random.normal(stream_key, shape, jnp.float32) * scale
    if len(shards) > 0:
        drawn = shard_levels(stream_key, shape, shards, -0.22, 0.18) * drawn
    return jnp.clip(drawn, min=-limit, max=limit).astype(kind)


def setup_inputs(seed: int = 0, part: int = 0) -> dict:
    key_of = jax.random.split(jax.random.key(seed), 7)
    part_keys = jax.random.split(jax.random.fold_in(key_of[6], part), 7)
    walkers = bell_draw(part_keys[0], (W, 2, M * N), 1.0, 6.0, ((0, 2), (2, 8)), jnp.float32)
    correlation_inverse = bell_draw(part_keys[1], (W, 2, N, N), N ** -0.5, 0.625, ((0, 2),), jnp.float32)
    half_vectors = bell_draw(part_keys[2], (G, M * N), (3 * M * N) ** -0.5, 0.01953125, ((0, 2), (1, 8)))
    field_vectors = bell_draw(part_keys[3], (G, M, M), (2 * G * M) ** -0.5, 0.0048828125, ((0, 2), (1, 8)))
    samples = bell_draw(part_keys[4], (W, G), 1.0, 6.0, ((1, 2),), jnp.float32)
    source = touch_ends(ranked(part_keys[5], (W,), W, 2), jax.random.fold_in(part_keys[5], 3), 0, W - 1).astype(jnp.int32)
    return dict(walkers=walkers, correlation_inverse=correlation_inverse, half_vectors=half_vectors, field_vectors=field_vectors, samples=samples, source=source)


def to_half(value):
    return lax.optimization_barrier(value.astype(jnp.bfloat16)).astype(jnp.float32)

def complex_product(left_real, left_imag, right_real, right_imag, formula):
    first = jnp.einsum(formula, left_real, right_real, precision=lax.Precision.HIGHEST)
    second = jnp.einsum(formula, left_imag, right_imag, precision=lax.Precision.HIGHEST)
    third = jnp.einsum(formula, left_real, right_imag, precision=lax.Precision.HIGHEST)
    fourth = jnp.einsum(formula, left_imag, right_real, precision=lax.Precision.HIGHEST)
    return (first - second, third + fourth)

def normalizer(gram_real, gram_imag):
    electrons = gram_real.shape[-1]
    identity = jnp.eye(electrons, dtype=jnp.float32)
    scale_factor = jnp.trace(gram_real, axis1=1, axis2=2) / electrons
    iter_real = gram_real / scale_factor[:, None, None]
    iter_imag = gram_imag / scale_factor[:, None, None]
    root_real = jnp.broadcast_to(identity, gram_real.shape)
    root_imag = jnp.zeros_like(gram_real)
    for sweep_index in range(NS_STEPS):
        prod_real, prod_imag = complex_product(root_real, root_imag, iter_real, iter_imag, 'wij,wjk->wik')
        step_real = 1.5 * identity - 0.5 * prod_real
        step_imag = -0.5 * prod_imag
        iter_real, iter_imag = complex_product(iter_real, iter_imag, step_real, step_imag, 'wij,wjk->wik')
        root_real, root_imag = complex_product(step_real, step_imag, root_real, root_imag, 'wij,wjk->wik')
    inverse_root = lax.rsqrt(scale_factor)[:, None, None]
    return (root_real * inverse_root, root_imag * inverse_root)

def reference(walkers, correlation_inverse, half_vectors, field_vectors, samples, source):
    population = walkers.shape[0]
    grid = walkers.reshape(population, 2, M, N)
    theta_real, theta_imag = complex_product(grid[:, 0], grid[:, 1], correlation_inverse[:, 0], correlation_inverse[:, 1], 'wmk,wkn->wmn')
    theta = to_half(jnp.stack([theta_real, theta_imag], 1).reshape(population, 2, M * N))
    bias = jnp.einsum('wcj,gj->wcg', theta, half_vectors.astype(jnp.float32), precision=lax.Precision.HIGHEST)
    coefficient = to_half(jnp.stack([bias[:, 1], samples - bias[:, 0]], 1))
    field = jnp.einsum('wcg,gab->wcab', coefficient, field_vectors.astype(jnp.float32), precision=lax.Precision.HIGHEST)
    field = to_half(field)
    field_real = field[:, 0]
    field_imag = field[:, 1]
    current = grid
    summed = grid
    for order_index in range(1, TERMS + 1):
        rounded = to_half(current)
        next_real, next_imag = complex_product(field_real, field_imag, rounded[:, 0], rounded[:, 1], 'wab,wbn->wan')
        current = jnp.stack([next_real, next_imag], 1) / order_index
        summed = summed + current
    total_real = summed[:, 0]
    total_imag = summed[:, 1]
    gram_real, gram_imag = complex_product(total_real, -total_imag, total_real, total_imag, 'wmi,wmj->wij')
    gram_real = gram_real / M
    gram_imag = gram_imag / M
    root_real, root_imag = normalizer(gram_real, gram_imag)
    norm_real, norm_imag = complex_product(total_real, total_imag, root_real, root_imag, 'wmk,wkn->wmn')
    normalized = jnp.stack([norm_real, norm_imag], 1).reshape(population, 2, M * N)
    return jnp.take(normalized, source.astype(jnp.int32), axis=0)
```

```python
import functools

import jax
import jax.numpy as jnp
from jax import lax
from jax.experimental import pallas as pl
from jax.experimental.pallas import tpu as pltpu
from jax.sharding import PartitionSpec as P

TERMS = 4
NS_STEPS = 2


def for_sending(shard):
    return jax.tree.map(lambda a: a.astype(jnp.bfloat16) if a.dtype == jnp.float32 else a, shard)


def complex_product(left_real, left_imag, right_real, right_imag, formula):
    first = jnp.einsum(formula, left_real, right_real, precision=lax.Precision.HIGHEST)
    second = jnp.einsum(formula, left_imag, right_imag, precision=lax.Precision.HIGHEST)
    third = jnp.einsum(formula, left_real, right_imag, precision=lax.Precision.HIGHEST)
    fourth = jnp.einsum(formula, left_imag, right_real, precision=lax.Precision.HIGHEST)
    return (first - second, third + fourth)


def normalizer(gram_real, gram_imag):
    electrons = gram_real.shape[-1]
    identity = jnp.eye(electrons, dtype=jnp.float32)
    scale_factor = jnp.trace(gram_real, axis1=1, axis2=2) / electrons
    iter_real = gram_real / scale_factor[:, None, None]
    iter_imag = gram_imag / scale_factor[:, None, None]
    root_real = jnp.broadcast_to(identity, gram_real.shape)
    root_imag = jnp.zeros_like(gram_real)
    for sweep_index in range(NS_STEPS):
        prod_real, prod_imag = complex_product(
            root_real, root_imag, iter_real, iter_imag, "wij,wjk->wik"
        )
        step_real = 1.5 * identity - 0.5 * prod_real
        step_imag = -0.5 * prod_imag
        iter_real, iter_imag = complex_product(
            iter_real, iter_imag, step_real, step_imag, "wij,wjk->wik"
        )
        root_real, root_imag = complex_product(
            step_real, step_imag, root_real, root_imag, "wij,wjk->wik"
        )
    inverse_root = lax.rsqrt(scale_factor)[:, None, None]
    return (root_real * inverse_root, root_imag * inverse_root)


def field_apply(field_block, values):
    next_real = jnp.einsum(
        "wab,wbn->wan", field_block[:, 0], values[:, 0], preferred_element_type=jnp.float32
    )
    next_real = next_real - jnp.einsum(
        "wab,wbn->wan", field_block[:, 1], values[:, 1], preferred_element_type=jnp.float32
    )
    next_imag = jnp.einsum(
        "wab,wbn->wan", field_block[:, 0], values[:, 1], preferred_element_type=jnp.float32
    )
    next_imag = next_imag + jnp.einsum(
        "wab,wbn->wan", field_block[:, 1], values[:, 0], preferred_element_type=jnp.float32
    )
    return jnp.stack([next_real, next_imag], 1)


def plain_body(walkers, correlation_inverse, half_vectors, field_vectors, samples, source):
    local_walkers = walkers.shape[0]
    row_block = field_vectors.shape[1]
    orbitals = field_vectors.shape[2]
    electrons = correlation_inverse.shape[2]
    grid = walkers.reshape(local_walkers, 2, row_block, electrons)
    theta_real, theta_imag = complex_product(
        grid[:, 0], grid[:, 1], correlation_inverse[:, 0], correlation_inverse[:, 1], "wmk,wkn->wmn"
    )
    theta = (
        jnp.stack([theta_real, theta_imag], 1)
        .reshape(local_walkers, 2, row_block * electrons)
        .astype(jnp.bfloat16)
    )
    all_theta = lax.all_gather(theta, "walk", axis=0, tiled=True)
    bias_part = jnp.einsum(
        "wcj,gj->wcg", all_theta, half_vectors, preferred_element_type=jnp.float32
    )
    bias = lax.psum(bias_part, ("chol", "orb"))
    coefficient = jnp.stack([bias[:, 1], samples - bias[:, 0]], 1).astype(jnp.bfloat16)
    field_part = jnp.einsum(
        "wcg,gab->wcab", coefficient, field_vectors, preferred_element_type=jnp.float32
    )
    field = lax.psum_scatter(field_part, "walk", scatter_dimension=0, tiled=True).astype(
        jnp.bfloat16
    )
    devices_rows = lax.axis_size(("chol", "orb"))
    sharers = devices_rows // local_walkers
    col_width = electrons // sharers
    parted = grid.reshape(local_walkers, 2, row_block, sharers, col_width)
    parted = parted.transpose(0, 3, 1, 2, 4).reshape(devices_rows, 2, row_block, col_width)
    columns = lax.all_to_all(
        parted.astype(jnp.bfloat16), ("chol", "orb"), split_axis=0, concat_axis=2, tiled=True
    ).astype(parted.dtype)
    spread = jnp.broadcast_to(field[:, None], (local_walkers, sharers, 2, row_block, orbitals))
    spread = spread.reshape(devices_rows, 2, row_block, orbitals)
    whole_field = lax.all_to_all(spread, ("chol", "orb"), split_axis=0, concat_axis=2, tiled=True)
    current = columns
    col_summed = columns
    for order_index in range(1, TERMS + 1):
        current = field_apply(whole_field, current.astype(jnp.bfloat16)) / order_index
        col_summed = col_summed + current
    returned = lax.all_to_all(
        col_summed.astype(jnp.bfloat16), ("chol", "orb"), split_axis=2, concat_axis=0, tiled=True
    ).astype(col_summed.dtype)
    returned = returned.reshape(local_walkers, sharers, 2, row_block, col_width)
    summed = returned.transpose(0, 2, 3, 1, 4).reshape(local_walkers, 2, row_block, electrons)
    whole = lax.all_gather(summed.astype(jnp.bfloat16), ("chol", "orb"), axis=2, tiled=True).astype(
        summed.dtype
    )
    gram_real, gram_imag = complex_product(
        whole[:, 0], -whole[:, 1], whole[:, 0], whole[:, 1], "wmi,wmj->wij"
    )
    gram_real = gram_real / orbitals
    gram_imag = gram_imag / orbitals
    root_real, root_imag = normalizer(gram_real, gram_imag)
    norm_real, norm_imag = complex_product(
        summed[:, 0], summed[:, 1], root_real, root_imag, "wmk,wkn->wmn"
    )
    normalized = jnp.stack([norm_real, norm_imag], 1).reshape(
        local_walkers, 2, row_block * electrons
    )
    moved = lax.all_gather(for_sending(normalized), "walk", axis=0, tiled=True).astype(
        normalized.dtype
    )
    return jnp.take(moved, source, axis=0)


MESH = pl.DeviceIdType.MESH
LANES = 128
HALF = 8
ROWS = 16
VECTORS = 64
DEPTH = 4
VMEM_LIMIT = 48 * 1024 * 1024


def owner_id(index):
    orbs = lax.axis_size("orb")
    return {"chol": index // orbs, "orb": lax.rem(index, orbs)}


def position():
    return lax.axis_index("chol") * lax.axis_size("orb") + lax.axis_index("orb")


def greet(devices):
    barrier = pltpu.get_barrier_semaphore()
    for device in devices:
        pl.semaphore_signal(barrier, inc=1, device_id=device, device_id_type=MESH)
    pl.semaphore_wait(barrier, len(devices))


def cross(count, sharers):
    me, walk = position(), lax.axis_index("walk")
    rows = [owner_id(lax.rem(me + step, count)) for step in range(1, count)]
    return rows + [{"walk": lax.rem(walk + step, sharers)} for step in range(1, sharers)]


def remote(source, target, send, recv, device):
    return pltpu.make_async_remote_copy(
        src_ref=source, dst_ref=target, send_sem=send, recv_sem=recv,
        device_id=device, device_id_type=MESH,
    )


def bias_kernel(count, sharers, theta_ref, half_ref, samples_ref, coef_ref,
                half, theta, parts, arrived, load_sem, theta_send, theta_recv,
                part_send, part_recv, coef_send, coef_recv):
    me, walk = position(), lax.axis_index("walk")
    width = half.shape[1]
    local = theta_ref.shape[0] // 2

    def load(index):
        return pltpu.make_async_copy(
            half_ref.at[pl.ds(pl.multiple_of(index * width, width), width), :],
            half.at[index], load_sem.at[index],
        )

    def first(step, carry):
        load(lax.rem(me + 1 + step, count)).start()
        return carry

    lax.fori_loop(0, count, first, 0)
    greet(cross(count, sharers))
    sends = []
    for step in range(1, sharers):
        other = lax.rem(walk + step, sharers)
        sends.append(remote(theta_ref, theta.at[walk], theta_send.at[step],
                            theta_recv.at[walk], {"walk": other}))
        sends[-1].start()
    theta[walk] = theta_ref[...]
    for step in range(1, sharers):
        other = lax.rem(walk + step, sharers)
        remote(theta_ref, theta.at[other], theta_send.at[step],
               theta_recv.at[other], {"walk": other}).wait_recv()

    def product(index):
        load(index).wait()
        return lax.dot_general(
            theta[...].reshape(sharers * 2 * local, theta.shape[2]), half[index],
            (((1,), (1,)), ((), ())), preferred_element_type=jnp.float32,
        )

    def part_copy(index):
        return remote(parts.at[index], arrived.at[me], part_send.at[index],
                      part_recv.at[me], owner_id(index))

    def one(step, carry):
        index = lax.rem(me + 1 + step, count)
        parts[index] = product(index)
        part_copy(index).start()
        return carry

    lax.fori_loop(0, count - 1, one, 0)
    arrived[me] = product(me)

    def take(step, carry):
        index = lax.rem(me + 1 + step, count)
        remote(parts.at[index], arrived.at[index], part_send.at[index],
               part_recv.at[index], owner_id(index)).wait_recv()
        return carry

    lax.fori_loop(0, count - 1, take, 0)
    bias = jnp.sum(arrived[...], axis=0).reshape(sharers, 2, local, width)
    chosen = samples_ref[:, pl.ds(pl.multiple_of(me * width, width), width)]
    chosen = chosen.reshape(sharers, local, width)
    pair = jnp.stack([bias[:, 1], chosen - bias[:, 0]], 1)
    coef_ref[me] = pair.reshape(sharers * 2 * local, width).astype(jnp.bfloat16)

    def spread(step, carry):
        index = lax.rem(me + 1 + step, count)
        remote(coef_ref.at[me], coef_ref.at[me], coef_send.at[index],
               coef_recv.at[me], owner_id(index)).start()
        return carry

    lax.fori_loop(0, count - 1, spread, 0)

    def finish(step, carry):
        index = lax.rem(me + 1 + step, count)
        part_copy(index).wait_send()
        remote(coef_ref.at[me], coef_ref.at[index], coef_send.at[index],
               coef_recv.at[index], owner_id(index)).wait()
        return carry

    lax.fori_loop(0, count - 1, finish, 0)
    for send in sends:
        send.wait_send()


def field_kernel(count, sharers, coef_ref, columns_ref, vectors_ref, field_ref, whole_ref,
                 spread, blocks, total, full, outgoing, incoming, finished,
                 load_sem, column_send, column_recv, walk_send, walk_recv,
                 row_send, row_recv):
    me, walk = position(), lax.axis_index("walk")
    local = columns_ref.shape[0]
    row_block = columns_ref.shape[1]
    orbitals = vectors_ref.shape[2]
    chunks = vectors_ref.shape[0] // VECTORS
    groups = row_block // ROWS
    lines = coef_ref.shape[1]
    per_block = coef_ref.shape[2] // VECTORS
    depth = VECTORS * HALF

    def load(step):
        group, chunk = step // chunks, lax.rem(step, chunks)
        slot = lax.rem(step, DEPTH)
        return pltpu.make_async_copy(
            vectors_ref.at[pl.ds(pl.multiple_of(chunk * VECTORS, VECTORS), VECTORS),
                           pl.ds(pl.multiple_of(group * ROWS, ROWS), ROWS), :],
            blocks.at[slot], load_sem.at[slot],
        )

    for step in range(DEPTH - 1):
        load(jnp.int32(step)).start()
    greet(cross(count, sharers))
    here = pl.ds(pl.multiple_of(me * row_block, ROWS), row_block)

    def column_copy(index):
        return remote(columns_ref.at[index], whole_ref.at[here, :], column_send.at[index],
                      column_recv.at[me], owner_id(index))

    def send_columns(step, carry):
        column_copy(lax.rem(me + 1 + step, count)).start()
        return carry

    lax.fori_loop(0, count - 1, send_columns, 0)
    whole_ref[here, :] = columns_ref[me]

    vector_at = lax.broadcasted_iota(jnp.int32, (LANES, depth), 0)
    place = lax.broadcasted_iota(jnp.int32, (LANES, depth), 1)
    row_at = lax.broadcasted_iota(jnp.int32, (HALF, depth), 0)
    row_place = lax.broadcasted_iota(jnp.int32, (HALF, depth), 1)
    diagonal = (lax.rem(row_place, HALF) == row_at).astype(jnp.float32)

    for part in range(per_block):
        picks = (vector_at == place // HALF + part * VECTORS).astype(jnp.bfloat16)

        def widen(block, carry):
            repeated = jnp.dot(coef_ref[block], picks, preferred_element_type=jnp.float32)
            wide = repeated[:, None, :] * diagonal[None]
            spread[block * per_block + part] = wide.reshape(lines * HALF, depth).astype(
                jnp.bfloat16
            )
            return carry

        lax.fori_loop(0, coef_ref.shape[0], widen, 0)

    def walk_copy(group, step, arriving):
        other = lax.rem(walk + step, sharers) if not arriving else lax.rem(
            walk + sharers - step, sharers)
        return remote(outgoing.at[group, other], incoming.at[group, other if arriving else walk],
                      walk_send.at[group, other], walk_recv.at[group, other if arriving else walk],
                      {"walk": other})

    def row_copy(group, index, arriving):
        giver = index if arriving else me
        at = pl.ds(pl.multiple_of(giver * row_block + group * ROWS, ROWS), ROWS)
        return remote(finished.at[group, index], field_ref.at[:, at, :],
                      row_send.at[group, index], row_recv.at[group, giver], owner_id(index))

    def deliver(group):
        result = full[group, walk]
        for step in range(1, sharers):
            walk_copy(group, step, True).wait_recv()
            other = lax.rem(walk + sharers - step, sharers)
            result = result + incoming[group, other].astype(jnp.float32)
        finished[group] = result.astype(jnp.bfloat16)

        def send_rows(step, carry):
            row_copy(group, lax.rem(me + 1 + step, count), False).start()
            return carry

        lax.fori_loop(0, count - 1, send_rows, 0)
        field_ref[:, pl.ds(pl.multiple_of(me * row_block + group * ROWS, ROWS), ROWS), :] = (
            finished[group, me]
        )

    for group in range(groups):
        total[...] = jnp.zeros_like(total)

        def add(chunk, carry):
            step = group * chunks + chunk

            @pl.when(step + DEPTH - 1 < groups * chunks)
            def _():
                load(step + DEPTH - 1).start()

            load(step).wait()
            block = blocks[lax.rem(step, DEPTH)]
            upper = block[:, :HALF, :].reshape(depth, orbitals)
            lower = block[:, HALF:, :].reshape(depth, orbitals)
            total[...] += jnp.dot(
                spread[chunk], jnp.concatenate([upper, lower], axis=1),
                preferred_element_type=jnp.float32,
            )
            return carry

        lax.fori_loop(0, chunks, add, 0)
        result = total[...].reshape(sharers, 2, local, HALF, 2 * orbitals)
        result = jnp.concatenate([result[..., :orbitals], result[..., orbitals:]], axis=3)
        for part in range(2):
            full[group, :, :, part] = result[:, part]
            outgoing[group, :, :, part] = result[:, part].astype(jnp.bfloat16)
        for step in range(1, sharers):
            walk_copy(group, step, False).start()
        if group > 0:
            deliver(group - 1)
    deliver(groups - 1)

    def finish(step, carry):
        index = lax.rem(me + 1 + step, count)
        column_copy(index).wait_send()
        there = pl.ds(pl.multiple_of(index * row_block, ROWS), row_block)
        remote(columns_ref.at[index], whole_ref.at[there, :], column_send.at[index],
               column_recv.at[index], owner_id(index)).wait_recv()
        for group in range(groups):
            row_copy(group, index, False).wait_send()
            row_copy(group, index, True).wait_recv()
        return carry

    lax.fori_loop(0, count - 1, finish, 0)
    for group in range(groups):
        for step in range(1, sharers):
            walk_copy(group, step, False).wait_send()


def exact(left, right, dims=(((1,), (0,)), ((), ()))):
    return lax.dot_general(left, right, dims, precision=lax.Precision.HIGHEST,
                           preferred_element_type=jnp.float32)


def walker_kernel(count, sharers, electrons, field_ref, whole_ref, out_ref,
                  send_sem, recv_sem, rows):
    me, walk = position(), lax.axis_index("walk")
    row_block = rows.shape[1]
    orbitals = field_ref.shape[1]
    others = []
    for across in range(sharers):
        for step in range(count):
            if across + step > 0:
                target = owner_id(lax.rem(me + step, count))
                target["walk"] = lax.rem(walk + across, sharers)
                others.append((across, step, target))
    greet([target for _, _, target in others])

    def swap(value, sign):
        return jnp.concatenate([-sign * value[:, LANES:], sign * value[:, :LANES]], axis=1)

    current = whole_ref[...].astype(jnp.float32)
    summed = current
    for order_index in range(1, TERMS + 1):
        rounded = current.astype(jnp.bfloat16)
        real = jnp.dot(field_ref[0], rounded, preferred_element_type=jnp.float32)
        imag = jnp.dot(field_ref[1], rounded, preferred_element_type=jnp.float32)
        current = (real + swap(imag, 1.0)) / order_index
        summed = summed + current
    squares = exact(summed, summed, (((0,), (0,)), ((), ()))) / orbitals
    gram_real = squares[:LANES, :LANES] + squares[LANES:, LANES:]
    gram_imag = squares[:LANES, LANES:] - squares[LANES:, :LANES]
    size = 2 * LANES
    identity = (
        lax.broadcasted_iota(jnp.int32, (size, size), 0)
        == lax.broadcasted_iota(jnp.int32, (size, size), 1)
    ).astype(jnp.float32)
    scale = jnp.sum(gram_real * identity[:LANES, :LANES]) / electrons
    top = jnp.concatenate([gram_real, gram_imag], axis=1)
    bottom = jnp.concatenate([-gram_imag, gram_real], axis=1)
    iterate = jnp.concatenate([top, bottom], axis=0) / scale
    step_of = 1.5 * identity - 0.5 * iterate
    root = step_of
    for sweep_index in range(1, NS_STEPS):
        iterate = exact(iterate, step_of)
        step_of = 1.5 * identity - 0.5 * exact(root, iterate)
        root = exact(step_of, root)
    normalized = exact(summed, root * lax.rsqrt(scale))
    rows[...] = normalized.reshape(count, row_block, size).astype(jnp.bfloat16)

    mine = walk * count + me
    for across, step, target in others:
        index = lax.rem(me + step, count)
        remote(rows.at[index], out_ref.at[mine], send_sem.at[across, step],
               recv_sem.at[across, step], target).start()
    out_ref[mine] = rows[me]
    for across, step, target in others:
        index = lax.rem(me + step, count)
        giver = lax.rem(walk + sharers - across, sharers) * count + lax.rem(
            me + count - step, count)
        remote(rows.at[index], out_ref.at[giver], send_sem.at[across, step],
               recv_sem.at[across, step], target).wait()


def call(kernel, ident, shapes, places, scratch):
    single = isinstance(shapes, jax.ShapeDtypeStruct)
    spec = pl.BlockSpec(memory_space=pltpu.VMEM)
    return pl.pallas_call(
        kernel,
        out_shape=shapes,
        in_specs=[pl.BlockSpec(memory_space=place) for place in places],
        out_specs=spec if single else [spec] * len(shapes),
        scratch_shapes=scratch,
        compiler_params=pltpu.CompilerParams(
            collective_id=ident, has_side_effects=True, vmem_limit_bytes=VMEM_LIMIT
        ),
    )


def body(walkers, correlation_inverse, half_vectors, field_vectors, samples, source):
    local_walkers = walkers.shape[0]
    vectors, row_block, orbitals = field_vectors.shape
    electrons = correlation_inverse.shape[2]
    flat = row_block * electrons
    count = lax.axis_size(("chol", "orb"))
    sharers = lax.axis_size("walk")
    width = vectors // count
    fits = (
        count == local_walkers and row_block % ROWS == 0 and local_walkers % HALF == 0
        and width % LANES == 0 and LANES % VECTORS == 0 and width == LANES
        and electrons <= LANES and orbitals % LANES == 0
    )
    if not fits:
        return plain_body(
            walkers, correlation_inverse, half_vectors, field_vectors, samples, source
        )
    lines = sharers * 2 * local_walkers
    groups = row_block // ROWS
    chunks = vectors // VECTORS
    vmem, anywhere = pltpu.VMEM, pl.ANY
    dma = pltpu.SemaphoreType.DMA
    half_type, full_type = jnp.bfloat16, jnp.float32
    grid = walkers.reshape(local_walkers, 2, row_block, electrons)
    theta_real, theta_imag = complex_product(
        grid[:, 0], grid[:, 1], correlation_inverse[:, 0], correlation_inverse[:, 1], "wmk,wkn->wmn"
    )
    theta = jnp.stack([theta_real, theta_imag], 0).astype(half_type)
    theta = theta.reshape(2 * local_walkers, flat)
    coefficient = call(
        functools.partial(bias_kernel, count, sharers), 0,
        jax.ShapeDtypeStruct((count, lines, width), half_type),
        [vmem, anywhere, vmem],
        [
            vmem((count, width, flat), half_type),
            vmem((sharers, 2 * local_walkers, flat), half_type),
            vmem((count, lines, width), full_type),
            vmem((count, lines, width), full_type),
            dma((count,)), dma((sharers,)), dma((sharers,)),
            dma((count,)), dma((count,)), dma((count,)), dma((count,)),
        ],
    )(theta, half_vectors, samples)
    columns = jnp.pad(grid.astype(half_type), ((0, 0), (0, 0), (0, 0), (0, LANES - electrons)))
    columns = columns.transpose(0, 2, 1, 3).reshape(local_walkers, row_block, 2 * LANES)
    field, whole = call(
        functools.partial(field_kernel, count, sharers), 1,
        [
            jax.ShapeDtypeStruct((2, orbitals, orbitals), half_type),
            jax.ShapeDtypeStruct((orbitals, 2 * LANES), half_type),
        ],
        [vmem, vmem, anywhere],
        [
            vmem((chunks, lines * HALF, VECTORS * HALF), half_type),
            vmem((DEPTH, VECTORS, ROWS, orbitals), half_type),
            vmem((lines * HALF, 2 * orbitals), full_type),
            vmem((groups, sharers, local_walkers, 2, ROWS, orbitals), full_type),
            vmem((groups, sharers, local_walkers, 2, ROWS, orbitals), half_type),
            vmem((groups, sharers, local_walkers, 2, ROWS, orbitals), half_type),
            vmem((groups, local_walkers, 2, ROWS, orbitals), half_type),
            dma((DEPTH,)), dma((count,)), dma((count,)),
            dma((groups, sharers)), dma((groups, sharers)),
            dma((groups, count)), dma((groups, count)),
        ],
    )(coefficient, columns, field_vectors)
    moved = call(
        functools.partial(walker_kernel, count, sharers, electrons), 2,
        jax.ShapeDtypeStruct((sharers * local_walkers, row_block, 2 * LANES), half_type),
        [vmem, vmem],
        [
            dma((sharers, count)), dma((sharers, count)),
            vmem((count, row_block, 2 * LANES), half_type),
        ],
    )(field, whole)
    chosen = jnp.take(moved, source, axis=0).reshape(local_walkers, row_block, 2, LANES)
    chosen = chosen[..., :electrons].transpose(0, 2, 1, 3)
    return chosen.reshape(local_walkers, 2, flat).astype(walkers.dtype)


def solution(mesh):
    placed = (
        P(("groups", "walk"), None, ("chol", "orb")),
        P(("groups", "walk"), None, None, None),
        P(("groups", "walk"), ("chol", "orb")),
        P(("groups", "walk"), ("chol", "orb"), None),
        P("groups", "walk"),
        P(("groups", "walk")),
    )
    return jax.shard_map(
        body,
        mesh=mesh,
        in_specs=placed,
        out_specs=P(("groups", "walk"), None, ("chol", "orb")),
        check_vma=False,
    )
```

```python
import functools

import jax
import jax.numpy as jnp
from jax import lax
from jax.experimental import pallas as pl
from jax.experimental.pallas import tpu as pltpu
from jax.sharding import PartitionSpec as P

TERMS = 4
NS_STEPS = 2


def for_sending(shard):
    return jax.tree.map(lambda a: a.astype(jnp.bfloat16) if a.dtype == jnp.float32 else a, shard)


def complex_product(left_real, left_imag, right_real, right_imag, formula):
    first = jnp.einsum(formula, left_real, right_real, precision=lax.Precision.HIGHEST)
    second = jnp.einsum(formula, left_imag, right_imag, precision=lax.Precision.HIGHEST)
    third = jnp.einsum(formula, left_real, right_imag, precision=lax.Precision.HIGHEST)
    fourth = jnp.einsum(formula, left_imag, right_real, precision=lax.Precision.HIGHEST)
    return (first - second, third + fourth)


def normalizer(gram_real, gram_imag):
    electrons = gram_real.shape[-1]
    identity = jnp.eye(electrons, dtype=jnp.float32)
    scale_factor = jnp.trace(gram_real, axis1=1, axis2=2) / electrons
    iter_real = gram_real / scale_factor[:, None, None]
    iter_imag = gram_imag / scale_factor[:, None, None]
    root_real = jnp.broadcast_to(identity, gram_real.shape)
    root_imag = jnp.zeros_like(gram_real)
    for sweep_index in range(NS_STEPS):
        prod_real, prod_imag = complex_product(
            root_real, root_imag, iter_real, iter_imag, "wij,wjk->wik"
        )
        step_real = 1.5 * identity - 0.5 * prod_real
        step_imag = -0.5 * prod_imag
        iter_real, iter_imag = complex_product(
            iter_real, iter_imag, step_real, step_imag, "wij,wjk->wik"
        )
        root_real, root_imag = complex_product(
            step_real, step_imag, root_real, root_imag, "wij,wjk->wik"
        )
    inverse_root = lax.rsqrt(scale_factor)[:, None, None]
    return (root_real * inverse_root, root_imag * inverse_root)


def field_apply(field_block, values):
    next_real = jnp.einsum(
        "wab,wbn->wan", field_block[:, 0], values[:, 0], preferred_element_type=jnp.float32
    )
    next_real = next_real - jnp.einsum(
        "wab,wbn->wan", field_block[:, 1], values[:, 1], preferred_element_type=jnp.float32
    )
    next_imag = jnp.einsum(
        "wab,wbn->wan", field_block[:, 0], values[:, 1], preferred_element_type=jnp.float32
    )
    next_imag = next_imag + jnp.einsum(
        "wab,wbn->wan", field_block[:, 1], values[:, 0], preferred_element_type=jnp.float32
    )
    return jnp.stack([next_real, next_imag], 1)


def plain_body(walkers, correlation_inverse, half_vectors, field_vectors, samples, source):
    local_walkers = walkers.shape[0]
    row_block = field_vectors.shape[1]
    orbitals = field_vectors.shape[2]
    electrons = correlation_inverse.shape[2]
    grid = walkers.reshape(local_walkers, 2, row_block, electrons)
    theta_real, theta_imag = complex_product(
        grid[:, 0], grid[:, 1], correlation_inverse[:, 0], correlation_inverse[:, 1], "wmk,wkn->wmn"
    )
    theta = (
        jnp.stack([theta_real, theta_imag], 1)
        .reshape(local_walkers, 2, row_block * electrons)
        .astype(jnp.bfloat16)
    )
    all_theta = lax.all_gather(theta, "walk", axis=0, tiled=True)
    bias_part = jnp.einsum(
        "wcj,gj->wcg", all_theta, half_vectors, preferred_element_type=jnp.float32
    )
    bias = lax.psum(bias_part, ("chol", "orb"))
    coefficient = jnp.stack([bias[:, 1], samples - bias[:, 0]], 1).astype(jnp.bfloat16)
    field_part = jnp.einsum(
        "wcg,gab->wcab", coefficient, field_vectors, preferred_element_type=jnp.float32
    )
    field = lax.psum_scatter(field_part, "walk", scatter_dimension=0, tiled=True).astype(
        jnp.bfloat16
    )
    devices_rows = lax.axis_size(("chol", "orb"))
    sharers = devices_rows // local_walkers
    col_width = electrons // sharers
    parted = grid.reshape(local_walkers, 2, row_block, sharers, col_width)
    parted = parted.transpose(0, 3, 1, 2, 4).reshape(devices_rows, 2, row_block, col_width)
    columns = lax.all_to_all(
        parted.astype(jnp.bfloat16), ("chol", "orb"), split_axis=0, concat_axis=2, tiled=True
    ).astype(parted.dtype)
    spread = jnp.broadcast_to(field[:, None], (local_walkers, sharers, 2, row_block, orbitals))
    spread = spread.reshape(devices_rows, 2, row_block, orbitals)
    whole_field = lax.all_to_all(spread, ("chol", "orb"), split_axis=0, concat_axis=2, tiled=True)
    current = columns
    col_summed = columns
    for order_index in range(1, TERMS + 1):
        current = field_apply(whole_field, current.astype(jnp.bfloat16)) / order_index
        col_summed = col_summed + current
    returned = lax.all_to_all(
        col_summed.astype(jnp.bfloat16), ("chol", "orb"), split_axis=2, concat_axis=0, tiled=True
    ).astype(col_summed.dtype)
    returned = returned.reshape(local_walkers, sharers, 2, row_block, col_width)
    summed = returned.transpose(0, 2, 3, 1, 4).reshape(local_walkers, 2, row_block, electrons)
    whole = lax.all_gather(summed.astype(jnp.bfloat16), ("chol", "orb"), axis=2, tiled=True).astype(
        summed.dtype
    )
    gram_real, gram_imag = complex_product(
        whole[:, 0], -whole[:, 1], whole[:, 0], whole[:, 1], "wmi,wmj->wij"
    )
    gram_real = gram_real / orbitals
    gram_imag = gram_imag / orbitals
    root_real, root_imag = normalizer(gram_real, gram_imag)
    norm_real, norm_imag = complex_product(
        summed[:, 0], summed[:, 1], root_real, root_imag, "wmk,wkn->wmn"
    )
    normalized = jnp.stack([norm_real, norm_imag], 1).reshape(
        local_walkers, 2, row_block * electrons
    )
    moved = lax.all_gather(for_sending(normalized), "walk", axis=0, tiled=True).astype(
        normalized.dtype
    )
    return jnp.take(moved, source, axis=0)


MESH = pl.DeviceIdType.MESH
LANES = 128
HALF = 8
ROWS = 16
VECTORS = 64
DEPTH = 32
VMEM_LIMIT = 60 * 1024 * 1024


def owner_id(index):
    orbs = lax.axis_size("orb")
    return {"chol": index // orbs, "orb": lax.rem(index, orbs)}


def position():
    return lax.axis_index("chol") * lax.axis_size("orb") + lax.axis_index("orb")


def greet(devices):
    barrier = pltpu.get_barrier_semaphore()
    for device in devices:
        pl.semaphore_signal(barrier, inc=1, device_id=device, device_id_type=MESH)
    pl.semaphore_wait(barrier, len(devices))


def partners(count, sharers):
    me, walk = position(), lax.axis_index("walk")
    others = []
    for across in range(sharers):
        for step in range(count):
            if across + step > 0:
                target = owner_id(lax.rem(me + step, count))
                target["walk"] = lax.rem(walk + across, sharers)
                others.append((across, step, target))
    return others


def remote(source, target, send, recv, device):
    return pltpu.make_async_remote_copy(
        src_ref=source, dst_ref=target, send_sem=send, recv_sem=recv,
        device_id=device, device_id_type=MESH,
    )


def half_load(half_ref, half, load_sem, index):
    width = half.shape[1]
    return pltpu.make_async_copy(
        half_ref.at[pl.ds(pl.multiple_of(index * width, width), width), :],
        half.at[index], load_sem.at[index],
    )


def block_load(vectors_ref, blocks, load_sem, step):
    chunks = vectors_ref.shape[0] // VECTORS
    group, chunk = step // chunks, lax.rem(step, chunks)
    slot = lax.rem(step, DEPTH)
    return pltpu.make_async_copy(
        vectors_ref.at[pl.ds(pl.multiple_of(chunk * VECTORS, VECTORS), VECTORS),
                       pl.ds(pl.multiple_of(group * ROWS, ROWS), ROWS), :],
        blocks.at[slot], load_sem.at[slot],
    )


def column_phase(count, columns_ref, whole_ref, column_send, column_recv):
    me = position()
    row_block = columns_ref.shape[1]
    here = pl.ds(pl.multiple_of(me * row_block, ROWS), row_block)

    def send_columns(step, carry):
        index = lax.rem(me + 1 + step, count)
        remote(columns_ref.at[index], whole_ref.at[here, :], column_send.at[index],
               column_recv.at[me], owner_id(index)).start()
        return carry

    lax.fori_loop(0, count - 1, send_columns, 0)
    whole_ref[here, :] = columns_ref[me]


def bias_phase(count, sharers, theta_ref, half_ref, samples_ref, coef_ref,
                half, theta, parts, arrived, load_sem, theta_send, theta_recv,
                part_send, part_recv, coef_send, coef_recv):
    me, walk = position(), lax.axis_index("walk")
    width = half.shape[1]
    local = theta_ref.shape[0] // 2

    def load(index):
        return half_load(half_ref, half, load_sem, index)

    sends = []
    for step in range(1, sharers):
        other = lax.rem(walk + step, sharers)
        sends.append(remote(theta_ref, theta.at[walk], theta_send.at[step],
                            theta_recv.at[walk], {"walk": other}))
        sends[-1].start()
    theta[walk] = theta_ref[...]
    for step in range(1, sharers):
        other = lax.rem(walk + step, sharers)
        remote(theta_ref, theta.at[other], theta_send.at[step],
               theta_recv.at[other], {"walk": other}).wait_recv()

    def product(index):
        load(index).wait()
        return lax.dot_general(
            theta[...].reshape(sharers * 2 * local, theta.shape[2]), half[index],
            (((1,), (1,)), ((), ())), preferred_element_type=jnp.float32,
        )

    def part_copy(index):
        return remote(parts.at[index], arrived.at[me], part_send.at[index],
                      part_recv.at[me], owner_id(index))

    def one(step, carry):
        index = lax.rem(me + 1 + step, count)
        parts[index] = product(index)
        part_copy(index).start()
        return carry

    lax.fori_loop(0, count - 1, one, 0)
    arrived[me] = product(me)

    def take(step, carry):
        index = lax.rem(me + 1 + step, count)
        remote(parts.at[index], arrived.at[index], part_send.at[index],
               part_recv.at[index], owner_id(index)).wait_recv()
        return carry

    lax.fori_loop(0, count - 1, take, 0)
    bias = jnp.sum(arrived[...], axis=0).reshape(sharers, 2, local, width)
    chosen = samples_ref[:, pl.ds(pl.multiple_of(me * width, width), width)]
    chosen = chosen.reshape(sharers, local, width)
    pair = jnp.stack([bias[:, 1], chosen - bias[:, 0]], 1)
    coef_ref[me] = pair.reshape(sharers * 2 * local, width).astype(jnp.bfloat16)

    def spread(step, carry):
        index = lax.rem(me + 1 + step, count)
        remote(coef_ref.at[me], coef_ref.at[me], coef_send.at[index],
               coef_recv.at[me], owner_id(index)).start()
        return carry

    lax.fori_loop(0, count - 1, spread, 0)

    def finish(step, carry):
        index = lax.rem(me + 1 + step, count)
        part_copy(index).wait_send()
        remote(coef_ref.at[me], coef_ref.at[index], coef_send.at[index],
               coef_recv.at[index], owner_id(index)).wait()
        return carry

    lax.fori_loop(0, count - 1, finish, 0)
    for send in sends:
        send.wait_send()


def field_phase(count, sharers, coef_ref, columns_ref, vectors_ref, field_ref, whole_ref,
                 spread, blocks, total, full, outgoing, incoming, finished,
                 load_sem, column_send, column_recv, walk_send, walk_recv,
                 row_send, row_recv):
    me, walk = position(), lax.axis_index("walk")
    local = columns_ref.shape[0]
    row_block = columns_ref.shape[1]
    orbitals = vectors_ref.shape[2]
    chunks = vectors_ref.shape[0] // VECTORS
    groups = row_block // ROWS
    lines = coef_ref.shape[1]
    per_block = coef_ref.shape[2] // VECTORS
    depth = VECTORS * HALF

    def load(step):
        return block_load(vectors_ref, blocks, load_sem, step)

    vector_at = lax.broadcasted_iota(jnp.int32, (LANES, depth), 0)
    place = lax.broadcasted_iota(jnp.int32, (LANES, depth), 1)
    row_at = lax.broadcasted_iota(jnp.int32, (HALF, depth), 0)
    row_place = lax.broadcasted_iota(jnp.int32, (HALF, depth), 1)
    diagonal = (lax.rem(row_place, HALF) == row_at).astype(jnp.float32)

    for part in range(per_block):
        picks = (vector_at == place // HALF + part * VECTORS).astype(jnp.bfloat16)

        def widen(block, carry):
            repeated = jnp.dot(coef_ref[block], picks, preferred_element_type=jnp.float32)
            wide = repeated[:, None, :] * diagonal[None]
            spread[block * per_block + part] = wide.reshape(lines * HALF, depth).astype(
                jnp.bfloat16
            )
            return carry

        lax.fori_loop(0, coef_ref.shape[0], widen, 0)

    def walk_copy(group, step, arriving):
        other = lax.rem(walk + step, sharers) if not arriving else lax.rem(
            walk + sharers - step, sharers)
        return remote(outgoing.at[group, other], incoming.at[group, other if arriving else walk],
                      walk_send.at[group, other], walk_recv.at[group, other if arriving else walk],
                      {"walk": other})

    def row_copy(group, index, arriving):
        giver = index if arriving else me
        at = pl.ds(pl.multiple_of(giver * row_block + group * ROWS, ROWS), ROWS)
        return remote(finished.at[group, index], field_ref.at[:, at, :],
                      row_send.at[group, index], row_recv.at[group, giver], owner_id(index))

    def deliver(group):
        result = full[group, walk]
        for step in range(1, sharers):
            walk_copy(group, step, True).wait_recv()
            other = lax.rem(walk + sharers - step, sharers)
            result = result + incoming[group, other].astype(jnp.float32)
        finished[group] = result.astype(jnp.bfloat16)

        def send_rows(step, carry):
            row_copy(group, lax.rem(me + 1 + step, count), False).start()
            return carry

        lax.fori_loop(0, count - 1, send_rows, 0)
        field_ref[:, pl.ds(pl.multiple_of(me * row_block + group * ROWS, ROWS), ROWS), :] = (
            finished[group, me]
        )

    for group in range(groups):
        total[...] = jnp.zeros_like(total)

        def add(chunk, carry):
            step = group * chunks + chunk

            @pl.when(step + DEPTH - 1 < groups * chunks)
            def _():
                load(step + DEPTH - 1).start()

            load(step).wait()
            block = blocks[lax.rem(step, DEPTH)]
            upper = block[:, :HALF, :].reshape(depth, orbitals)
            lower = block[:, HALF:, :].reshape(depth, orbitals)
            total[...] += jnp.dot(
                spread[chunk], jnp.concatenate([upper, lower], axis=1),
                preferred_element_type=jnp.float32,
            )
            return carry

        lax.fori_loop(0, chunks, add, 0)
        result = total[...].reshape(sharers, 2, local, HALF, 2 * orbitals)
        result = jnp.concatenate([result[..., :orbitals], result[..., orbitals:]], axis=3)
        for part in range(2):
            full[group, :, :, part] = result[:, part]
            outgoing[group, :, :, part] = result[:, part].astype(jnp.bfloat16)
        for step in range(1, sharers):
            walk_copy(group, step, False).start()
        if group > 0:
            deliver(group - 1)
    deliver(groups - 1)

    def finish(step, carry):
        index = lax.rem(me + 1 + step, count)
        there = pl.ds(pl.multiple_of(index * row_block, ROWS), row_block)
        remote(columns_ref.at[index], whole_ref.at[there, :], column_send.at[index],
               column_recv.at[index], owner_id(index)).wait()
        for group in range(groups):
            row_copy(group, index, False).wait_send()
            row_copy(group, index, True).wait_recv()
        return carry

    lax.fori_loop(0, count - 1, finish, 0)
    for group in range(groups):
        for step in range(1, sharers):
            walk_copy(group, step, False).wait_send()


def two_parts(value):
    high = value.astype(jnp.bfloat16)
    return high, (value - high.astype(jnp.float32)).astype(jnp.bfloat16)


def exact(left, right, axis=1):
    left_high, left_low = two_parts(left)
    right_high, right_low = two_parts(right)
    return lax.dot_general(
        jnp.concatenate([left_high, left_low, left_high], axis=axis),
        jnp.concatenate([right_high, right_high, right_low], axis=0),
        (((axis,), (0,)), ((), ())), preferred_element_type=jnp.float32,
    )


def walker_phase(count, sharers, electrons, field_ref, whole_ref, out_ref,
                 send_sem, recv_sem, rows):
    me, walk = position(), lax.axis_index("walk")
    row_block = rows.shape[1]
    orbitals = field_ref.shape[1]
    others = partners(count, sharers)

    def swap(value, sign):
        return jnp.concatenate([-sign * value[:, LANES:], sign * value[:, :LANES]], axis=1)

    current = whole_ref[...].astype(jnp.float32)
    summed = current
    for order_index in range(1, TERMS + 1):
        rounded = current.astype(jnp.bfloat16)
        real = jnp.dot(field_ref[0], rounded, preferred_element_type=jnp.float32)
        imag = jnp.dot(field_ref[1], rounded, preferred_element_type=jnp.float32)
        current = (real + swap(imag, 1.0)) / order_index
        summed = summed + current
    squares = exact(summed, summed, 0) / orbitals
    gram_real = squares[:LANES, :LANES] + squares[LANES:, LANES:]
    gram_imag = squares[:LANES, LANES:] - squares[LANES:, :LANES]
    size = 2 * LANES
    identity = (
        lax.broadcasted_iota(jnp.int32, (size, size), 0)
        == lax.broadcasted_iota(jnp.int32, (size, size), 1)
    ).astype(jnp.float32)
    scale = jnp.sum(gram_real * identity[:LANES, :LANES]) / electrons
    top = jnp.concatenate([gram_real, gram_imag], axis=1)
    bottom = jnp.concatenate([-gram_imag, gram_real], axis=1)
    iterate = jnp.concatenate([top, bottom], axis=0) / scale
    step_of = 1.5 * identity - 0.5 * iterate
    root = step_of
    for sweep_index in range(1, NS_STEPS):
        iterate = exact(iterate, step_of)
        step_of = 1.5 * identity - 0.5 * exact(root, iterate)
        root = exact(step_of, root)
    normalized = exact(summed, root * lax.rsqrt(scale))
    rows[...] = normalized.reshape(count, row_block, size).astype(jnp.bfloat16)

    mine = walk * count + me
    for across, step, target in others:
        index = lax.rem(me + step, count)
        remote(rows.at[index], out_ref.at[mine], send_sem.at[across, step],
               recv_sem.at[across, step], target).start()
    out_ref[mine] = rows[me]
    for across, step, target in others:
        index = lax.rem(me + step, count)
        giver = lax.rem(walk + sharers - across, sharers) * count + lax.rem(
            me + count - step, count)
        remote(rows.at[index], out_ref.at[giver], send_sem.at[across, step],
               recv_sem.at[across, step], target).wait()


def step_kernel(count, sharers, electrons, theta_ref, half_ref, samples_ref, columns_ref,
                vectors_ref, out_ref, half, theta, parts, arrived, coef, field, whole, spread,
                blocks, total, full, outgoing, incoming, finished, rows, half_sem, block_sem,
                theta_send, theta_recv, part_send, part_recv, coef_send, coef_recv,
                column_send, column_recv, walk_send, walk_recv, row_send, row_recv,
                out_send, out_recv):
    me = position()

    def first_half(step, carry):
        half_load(half_ref, half, half_sem, lax.rem(me + 1 + step, count)).start()
        return carry

    lax.fori_loop(0, count, first_half, 0)

    def first_blocks(step, carry):
        block_load(vectors_ref, blocks, block_sem, step).start()
        return carry

    lax.fori_loop(0, DEPTH - 1, first_blocks, 0)
    greet([target for _, _, target in partners(count, sharers)])
    bias_phase(count, sharers, theta_ref, half_ref, samples_ref, coef, half, theta, parts,
               arrived, half_sem, theta_send, theta_recv, part_send, part_recv, coef_send,
               coef_recv)
    column_phase(count, columns_ref, whole, column_send, column_recv)
    field_phase(count, sharers, coef, columns_ref, vectors_ref, field, whole, spread, blocks,
                total, full, outgoing, incoming, finished, block_sem, column_send, column_recv,
                walk_send, walk_recv, row_send, row_recv)
    walker_phase(count, sharers, electrons, field, whole, out_ref, out_send, out_recv, rows)


def body(walkers, correlation_inverse, half_vectors, field_vectors, samples, source):
    local_walkers = walkers.shape[0]
    vectors, row_block, orbitals = field_vectors.shape
    electrons = correlation_inverse.shape[2]
    flat = row_block * electrons
    count = lax.axis_size(("chol", "orb"))
    sharers = lax.axis_size("walk")
    width = vectors // count
    fits = (
        count == local_walkers and row_block % ROWS == 0 and local_walkers % HALF == 0
        and width % LANES == 0 and LANES % VECTORS == 0 and width == LANES
        and electrons <= LANES and orbitals % LANES == 0
        and (row_block // ROWS) * (vectors // VECTORS) >= DEPTH
    )
    if not fits:
        return plain_body(
            walkers, correlation_inverse, half_vectors, field_vectors, samples, source
        )
    lines = sharers * 2 * local_walkers
    groups = row_block // ROWS
    chunks = vectors // VECTORS
    vmem, anywhere = pltpu.VMEM, pl.ANY
    dma = pltpu.SemaphoreType.DMA
    half_type, full_type = jnp.bfloat16, jnp.float32
    grid = walkers.reshape(local_walkers, 2, row_block, electrons)
    pairs = jnp.concatenate([grid[:, 0], grid[:, 1]], axis=2)
    inverse_real, inverse_imag = correlation_inverse[:, 0], correlation_inverse[:, 1]
    theta = jnp.stack(
        [
            jnp.einsum("wmk,wkn->wmn", pairs, jnp.concatenate(side, axis=1),
                       precision=lax.Precision.HIGH)
            for side in ((inverse_real, -inverse_imag), (inverse_imag, inverse_real))
        ],
        0,
    ).astype(half_type)
    theta = theta.reshape(2 * local_walkers, flat)
    columns = jnp.pad(grid.astype(half_type), ((0, 0), (0, 0), (0, 0), (0, LANES - electrons)))
    columns = columns.transpose(0, 2, 1, 3).reshape(local_walkers, row_block, 2 * LANES)
    moved = pl.pallas_call(
        functools.partial(step_kernel, count, sharers, electrons),
        out_shape=jax.ShapeDtypeStruct((sharers * local_walkers, row_block, 2 * LANES), half_type),
        in_specs=[
            pl.BlockSpec(memory_space=place) for place in (vmem, anywhere, vmem, vmem, anywhere)
        ],
        out_specs=pl.BlockSpec(memory_space=vmem),
        scratch_shapes=[
            vmem((count, width, flat), half_type),
            vmem((sharers, 2 * local_walkers, flat), half_type),
            vmem((count, lines, width), full_type),
            vmem((count, lines, width), full_type),
            vmem((count, lines, width), half_type),
            vmem((2, orbitals, orbitals), half_type),
            vmem((orbitals, 2 * LANES), half_type),
            vmem((chunks, lines * HALF, VECTORS * HALF), half_type),
            vmem((DEPTH, VECTORS, ROWS, orbitals), half_type),
            vmem((lines * HALF, 2 * orbitals), full_type),
            vmem((groups, sharers, local_walkers, 2, ROWS, orbitals), full_type),
            vmem((groups, sharers, local_walkers, 2, ROWS, orbitals), half_type),
            vmem((groups, sharers, local_walkers, 2, ROWS, orbitals), half_type),
            vmem((groups, local_walkers, 2, ROWS, orbitals), half_type),
            vmem((count, row_block, 2 * LANES), half_type),
            dma((count,)), dma((DEPTH,)),
            dma((sharers,)), dma((sharers,)),
            dma((count,)), dma((count,)), dma((count,)), dma((count,)),
            dma((count,)), dma((count,)),
            dma((groups, sharers)), dma((groups, sharers)),
            dma((groups, count)), dma((groups, count)),
            dma((sharers, count)), dma((sharers, count)),
        ],
        compiler_params=pltpu.CompilerParams(
            collective_id=0, has_side_effects=True, vmem_limit_bytes=VMEM_LIMIT
        ),
    )(theta, half_vectors, samples, columns, field_vectors)
    chosen = jnp.take(moved, source, axis=0).reshape(local_walkers, row_block, 2, LANES)
    chosen = chosen[..., :electrons].transpose(0, 2, 1, 3)
    return chosen.reshape(local_walkers, 2, flat).astype(walkers.dtype)


def solution(mesh):
    placed = (
        P(("groups", "walk"), None, ("chol", "orb")),
        P(("groups", "walk"), None, None, None),
        P(("groups", "walk"), ("chol", "orb")),
        P(("groups", "walk"), ("chol", "orb"), None),
        P("groups", "walk"),
        P(("groups", "walk")),
    )
    return jax.shard_map(
        body,
        mesh=mesh,
        in_specs=placed,
        out_specs=P(("groups", "walk"), None, ("chol", "orb")),
        check_vma=False,
    )
```

```python
import functools

import jax
import jax.numpy as jnp
from jax import lax
from jax.experimental import pallas as pl
from jax.experimental.pallas import tpu as pltpu
from jax.sharding import PartitionSpec as P

TERMS = 4
NS_STEPS = 2


def for_sending(shard):
    return jax.tree.map(lambda a: a.astype(jnp.bfloat16) if a.dtype == jnp.float32 else a, shard)


def complex_product(left_real, left_imag, right_real, right_imag, formula):
    first = jnp.einsum(formula, left_real, right_real, precision=lax.Precision.HIGHEST)
    second = jnp.einsum(formula, left_imag, right_imag, precision=lax.Precision.HIGHEST)
    third = jnp.einsum(formula, left_real, right_imag, precision=lax.Precision.HIGHEST)
    fourth = jnp.einsum(formula, left_imag, right_real, precision=lax.Precision.HIGHEST)
    return (first - second, third + fourth)


def normalizer(gram_real, gram_imag):
    electrons = gram_real.shape[-1]
    identity = jnp.eye(electrons, dtype=jnp.float32)
    scale_factor = jnp.trace(gram_real, axis1=1, axis2=2) / electrons
    iter_real = gram_real / scale_factor[:, None, None]
    iter_imag = gram_imag / scale_factor[:, None, None]
    root_real = jnp.broadcast_to(identity, gram_real.shape)
    root_imag = jnp.zeros_like(gram_real)
    for sweep_index in range(NS_STEPS):
        prod_real, prod_imag = complex_product(
            root_real, root_imag, iter_real, iter_imag, "wij,wjk->wik"
        )
        step_real = 1.5 * identity - 0.5 * prod_real
        step_imag = -0.5 * prod_imag
        iter_real, iter_imag = complex_product(
            iter_real, iter_imag, step_real, step_imag, "wij,wjk->wik"
        )
        root_real, root_imag = complex_product(
            step_real, step_imag, root_real, root_imag, "wij,wjk->wik"
        )
    inverse_root = lax.rsqrt(scale_factor)[:, None, None]
    return (root_real * inverse_root, root_imag * inverse_root)


def field_apply(field_block, values):
    next_real = jnp.einsum(
        "wab,wbn->wan", field_block[:, 0], values[:, 0], preferred_element_type=jnp.float32
    )
    next_real = next_real - jnp.einsum(
        "wab,wbn->wan", field_block[:, 1], values[:, 1], preferred_element_type=jnp.float32
    )
    next_imag = jnp.einsum(
        "wab,wbn->wan", field_block[:, 0], values[:, 1], preferred_element_type=jnp.float32
    )
    next_imag = next_imag + jnp.einsum(
        "wab,wbn->wan", field_block[:, 1], values[:, 0], preferred_element_type=jnp.float32
    )
    return jnp.stack([next_real, next_imag], 1)


def plain_body(walkers, correlation_inverse, half_vectors, field_vectors, samples, source):
    local_walkers = walkers.shape[0]
    row_block = field_vectors.shape[1]
    orbitals = field_vectors.shape[2]
    electrons = correlation_inverse.shape[2]
    grid = walkers.reshape(local_walkers, 2, row_block, electrons)
    theta_real, theta_imag = complex_product(
        grid[:, 0], grid[:, 1], correlation_inverse[:, 0], correlation_inverse[:, 1], "wmk,wkn->wmn"
    )
    theta = (
        jnp.stack([theta_real, theta_imag], 1)
        .reshape(local_walkers, 2, row_block * electrons)
        .astype(jnp.bfloat16)
    )
    all_theta = lax.all_gather(theta, "walk", axis=0, tiled=True)
    bias_part = jnp.einsum(
        "wcj,gj->wcg", all_theta, half_vectors, preferred_element_type=jnp.float32
    )
    bias = lax.psum(bias_part, ("chol", "orb"))
    coefficient = jnp.stack([bias[:, 1], samples - bias[:, 0]], 1).astype(jnp.bfloat16)
    field_part = jnp.einsum(
        "wcg,gab->wcab", coefficient, field_vectors, preferred_element_type=jnp.float32
    )
    field = lax.psum_scatter(field_part, "walk", scatter_dimension=0, tiled=True).astype(
        jnp.bfloat16
    )
    devices_rows = lax.axis_size(("chol", "orb"))
    sharers = devices_rows // local_walkers
    col_width = electrons // sharers
    parted = grid.reshape(local_walkers, 2, row_block, sharers, col_width)
    parted = parted.transpose(0, 3, 1, 2, 4).reshape(devices_rows, 2, row_block, col_width)
    columns = lax.all_to_all(
        parted.astype(jnp.bfloat16), ("chol", "orb"), split_axis=0, concat_axis=2, tiled=True
    ).astype(parted.dtype)
    spread = jnp.broadcast_to(field[:, None], (local_walkers, sharers, 2, row_block, orbitals))
    spread = spread.reshape(devices_rows, 2, row_block, orbitals)
    whole_field = lax.all_to_all(spread, ("chol", "orb"), split_axis=0, concat_axis=2, tiled=True)
    current = columns
    col_summed = columns
    for order_index in range(1, TERMS + 1):
        current = field_apply(whole_field, current.astype(jnp.bfloat16)) / order_index
        col_summed = col_summed + current
    returned = lax.all_to_all(
        col_summed.astype(jnp.bfloat16), ("chol", "orb"), split_axis=2, concat_axis=0, tiled=True
    ).astype(col_summed.dtype)
    returned = returned.reshape(local_walkers, sharers, 2, row_block, col_width)
    summed = returned.transpose(0, 2, 3, 1, 4).reshape(local_walkers, 2, row_block, electrons)
    whole = lax.all_gather(summed.astype(jnp.bfloat16), ("chol", "orb"), axis=2, tiled=True).astype(
        summed.dtype
    )
    gram_real, gram_imag = complex_product(
        whole[:, 0], -whole[:, 1], whole[:, 0], whole[:, 1], "wmi,wmj->wij"
    )
    gram_real = gram_real / orbitals
    gram_imag = gram_imag / orbitals
    root_real, root_imag = normalizer(gram_real, gram_imag)
    norm_real, norm_imag = complex_product(
        summed[:, 0], summed[:, 1], root_real, root_imag, "wmk,wkn->wmn"
    )
    normalized = jnp.stack([norm_real, norm_imag], 1).reshape(
        local_walkers, 2, row_block * electrons
    )
    moved = lax.all_gather(for_sending(normalized), "walk", axis=0, tiled=True).astype(
        normalized.dtype
    )
    return jnp.take(moved, source, axis=0)


MESH = pl.DeviceIdType.MESH
LANES = 128
HALF = 8
ROWS = 16
VECTORS = 128
DEPTH = 48
LAG = 2
VMEM_LIMIT = 60 * 1024 * 1024


def owner_id(index):
    orbs = lax.axis_size("orb")
    return {"chol": index // orbs, "orb": lax.rem(index, orbs)}


def position():
    return lax.axis_index("chol") * lax.axis_size("orb") + lax.axis_index("orb")


def greet(devices):
    barrier = pltpu.get_barrier_semaphore()
    for device in devices:
        pl.semaphore_signal(barrier, inc=1, device_id=device, device_id_type=MESH)
    return barrier


def partners(count, sharers):
    me, walk = position(), lax.axis_index("walk")
    others = []
    for across in range(sharers):
        for step in range(count):
            if across + step > 0:
                target = owner_id(lax.rem(me + step, count))
                target["walk"] = lax.rem(walk + across, sharers)
                others.append((across, step, target))
    return others


def remote(source, target, send, recv, device):
    return pltpu.make_async_remote_copy(
        src_ref=source, dst_ref=target, send_sem=send, recv_sem=recv,
        device_id=device, device_id_type=MESH,
    )


def piece_at(across, piece, base):
    rows = pl.ds(pl.multiple_of(base + (piece // across) * ROWS, ROWS), ROWS)
    return rows, pl.ds(pl.multiple_of(lax.rem(piece, across) * LANES, LANES), LANES)


def theta_phase(columns_ref, inverse_ref, theta, columns, matrix, grid):
    walk = lax.axis_index("walk")
    local, row_block = columns_ref.shape[0], columns_ref.shape[1]
    electrons = inverse_ref.shape[2]
    matrix[...] = jnp.zeros_like(matrix)
    for walker in range(local):
        real, imag = inverse_ref[walker, 0], inverse_ref[walker, 1]
        matrix[:electrons, :electrons] = real
        matrix[:electrons, LANES:LANES + electrons] = imag
        matrix[LANES:LANES + electrons, :electrons] = -imag
        matrix[LANES:LANES + electrons, LANES:LANES + electrons] = real
        rotated = exact(columns_ref[walker], matrix[...])
        grid[:, walker, :] = rotated[:, :LANES]
        grid[:, local + walker, :] = rotated[:, LANES:]
        columns[walker] = columns_ref[walker].astype(jnp.bfloat16)
    lane = lax.broadcasted_iota(jnp.int32, (2 * local, LANES), 1)
    for tile in range(row_block * electrons // LANES):
        start = tile * LANES
        value = None
        for row in range(start // electrons, (start + LANES - 1) // electrons + 1):
            moved = pltpu.roll(grid[row], row * electrons % LANES, 1)
            value = moved if value is None else jnp.where(
                lane < row * electrons - start, value, moved)
        theta[walk, :, start:start + LANES] = value.astype(jnp.bfloat16)


def half_load(half_ref, half, load_sem, index):
    width = half.shape[1]
    return pltpu.make_async_copy(
        half_ref.at[pl.ds(pl.multiple_of(index * width, width), width), :],
        half.at[index], load_sem.at[index],
    )


def block_load(vectors_ref, blocks, load_sem, step):
    chunks = vectors_ref.shape[0] // VECTORS
    rows, lanes = piece_at(vectors_ref.shape[2] // LANES, step // chunks, 0)
    chunk, slot = lax.rem(step, chunks), lax.rem(step, DEPTH)
    return pltpu.make_async_copy(
        vectors_ref.at[pl.ds(pl.multiple_of(chunk * VECTORS, VECTORS), VECTORS), rows, lanes],
        blocks.at[slot], load_sem.at[slot],
    )


def column_phase(count, columns_ref, whole_ref, column_send, column_recv):
    me = position()
    row_block = columns_ref.shape[1]
    here = pl.ds(pl.multiple_of(me * row_block, ROWS), row_block)

    def send_columns(step, carry):
        index = lax.rem(me + 1 + step, count)
        remote(columns_ref.at[index], whole_ref.at[here, :], column_send.at[index],
               column_recv.at[me], owner_id(index)).start()
        return carry

    lax.fori_loop(0, count - 1, send_columns, 0)
    whole_ref[here, :] = columns_ref[me]


def bias_phase(count, sharers, half_ref, samples_ref, coef_ref,
                half, theta, parts, arrived, load_sem, theta_send, theta_recv,
                part_send, part_recv, coef_send, coef_recv):
    me, walk = position(), lax.axis_index("walk")
    width = half.shape[1]
    local = theta.shape[1] // 2

    def load(index):
        return half_load(half_ref, half, load_sem, index)

    sends = []
    for step in range(1, sharers):
        other = lax.rem(walk + step, sharers)
        sends.append(remote(theta.at[walk], theta.at[walk], theta_send.at[step],
                            theta_recv.at[walk], {"walk": other}))
        sends[-1].start()
    for step in range(1, sharers):
        other = lax.rem(walk + step, sharers)
        remote(theta.at[walk], theta.at[other], theta_send.at[step],
               theta_recv.at[other], {"walk": other}).wait_recv()

    def product(index):
        load(index).wait()
        return lax.dot_general(
            theta[...].reshape(sharers * 2 * local, theta.shape[2]), half[index],
            (((1,), (1,)), ((), ())), preferred_element_type=jnp.float32,
        )

    def part_copy(index):
        return remote(parts.at[index], arrived.at[me], part_send.at[index],
                      part_recv.at[me], owner_id(index))

    def one(step, carry):
        index = lax.rem(me + 1 + step, count)
        parts[index] = product(index)
        part_copy(index).start()
        return carry

    lax.fori_loop(0, count - 1, one, 0)
    arrived[me] = product(me)

    def take(step, carry):
        index = lax.rem(me + 1 + step, count)
        remote(parts.at[index], arrived.at[index], part_send.at[index],
               part_recv.at[index], owner_id(index)).wait_recv()
        return carry

    lax.fori_loop(0, count - 1, take, 0)
    bias = jnp.sum(arrived[...], axis=0).reshape(sharers, 2, local, width)
    chosen = samples_ref[:, pl.ds(pl.multiple_of(me * width, width), width)]
    chosen = chosen.reshape(sharers, local, width)
    pair = jnp.stack([bias[:, 1], chosen - bias[:, 0]], 1)
    coef_ref[me] = pair.reshape(sharers * 2 * local, width).astype(jnp.bfloat16)

    def spread(step, carry):
        index = lax.rem(me + 1 + step, count)
        remote(coef_ref.at[me], coef_ref.at[me], coef_send.at[index],
               coef_recv.at[me], owner_id(index)).start()
        return carry

    lax.fori_loop(0, count - 1, spread, 0)

    def finish(step, carry):
        index = lax.rem(me + 1 + step, count)
        part_copy(index).wait_send()
        remote(coef_ref.at[me], coef_ref.at[index], coef_send.at[index],
               coef_recv.at[index], owner_id(index)).wait()
        return carry

    lax.fori_loop(0, count - 1, finish, 0)
    for send in sends:
        send.wait_send()


def field_phase(count, sharers, coef_ref, columns_ref, vectors_ref, field_ref, whole_ref,
                 spread, blocks, total, full, outgoing, incoming, finished,
                 load_sem, column_send, column_recv, walk_send, walk_recv,
                 row_send, row_recv):
    me, walk = position(), lax.axis_index("walk")
    local = columns_ref.shape[0]
    row_block = columns_ref.shape[1]
    orbitals = vectors_ref.shape[2]
    chunks = vectors_ref.shape[0] // VECTORS
    lines = coef_ref.shape[1]
    per_block = coef_ref.shape[2] // VECTORS
    depth = VECTORS * HALF
    across = orbitals // LANES
    pieces = (row_block // ROWS) * across

    def load(step):
        return block_load(vectors_ref, blocks, load_sem, step)

    vector_at = lax.broadcasted_iota(jnp.int32, (LANES, depth), 0)
    place = lax.broadcasted_iota(jnp.int32, (LANES, depth), 1)
    row_at = lax.broadcasted_iota(jnp.int32, (HALF, depth), 0)
    row_place = lax.broadcasted_iota(jnp.int32, (HALF, depth), 1)
    diagonal = (lax.rem(row_place, HALF) == row_at).astype(jnp.float32)

    for part in range(per_block):
        picks = (vector_at == place // HALF + part * VECTORS).astype(jnp.bfloat16)

        def widen(block, carry):
            repeated = jnp.dot(coef_ref[block], picks, preferred_element_type=jnp.float32)
            wide = repeated[:, None, :] * diagonal[None]
            spread[block * per_block + part] = wide.reshape(lines * HALF, depth).astype(
                jnp.bfloat16
            )
            return carry

        lax.fori_loop(0, coef_ref.shape[0], widen, 0)

    def walk_copy(piece, step, arriving):
        other = lax.rem(walk + (sharers - step if arriving else step), sharers)
        giver = other if arriving else walk
        return remote(outgoing.at[piece, other], incoming.at[piece, giver],
                      walk_send.at[piece, other], walk_recv.at[piece, giver], {"walk": other})

    def row_copy(piece, index, arriving):
        giver = index if arriving else me
        rows, lanes = piece_at(across, piece, giver * row_block)
        return remote(finished.at[piece, index], field_ref.at[:, rows, lanes],
                      row_send.at[piece, index], row_recv.at[piece, giver], owner_id(index))

    def deliver(piece):
        result = full[piece, walk]
        for step in range(1, sharers):
            walk_copy(piece, step, True).wait_recv()
            other = lax.rem(walk + sharers - step, sharers)
            result = result + incoming[piece, other].astype(jnp.float32)
        finished[piece] = result.astype(jnp.bfloat16)

        def send_rows(step, carry):
            row_copy(piece, lax.rem(me + 1 + step, count), False).start()
            return carry

        lax.fori_loop(0, count - 1, send_rows, 0)
        rows, lanes = piece_at(across, piece, me * row_block)
        field_ref[:, rows, lanes] = finished[piece, me]

    def one_piece(piece, carry):
        total[...] = jnp.zeros_like(total)

        def add(chunk, inner):
            step = piece * chunks + chunk

            @pl.when(step + DEPTH - 1 < pieces * chunks)
            def _():
                load(step + DEPTH - 1).start()

            load(step).wait()
            block = blocks[lax.rem(step, DEPTH)]
            upper = block[:, :HALF, :].reshape(depth, LANES)
            lower = block[:, HALF:, :].reshape(depth, LANES)
            total[...] += jnp.dot(
                spread[chunk], jnp.concatenate([upper, lower], axis=1),
                preferred_element_type=jnp.float32,
            )
            return inner

        lax.fori_loop(0, chunks, add, 0)
        result = total[...].reshape(sharers, 2, local, HALF, 2 * LANES)
        result = jnp.concatenate([result[..., :LANES], result[..., LANES:]], axis=3)
        for part in range(2):
            full[piece, :, :, part] = result[:, part]
            outgoing[piece, :, :, part] = result[:, part].astype(jnp.bfloat16)
        for step in range(1, sharers):
            walk_copy(piece, step, False).start()

        @pl.when(piece >= LAG)
        def _():
            deliver(piece - LAG)

        return carry

    lax.fori_loop(0, pieces, one_piece, 0)
    for piece in range(pieces - LAG, pieces):
        deliver(piece)

    def finish(step, carry):
        index = lax.rem(me + 1 + step, count)
        there = pl.ds(pl.multiple_of(index * row_block, ROWS), row_block)
        remote(columns_ref.at[index], whole_ref.at[there, :], column_send.at[index],
               column_recv.at[index], owner_id(index)).wait()

        def pieces_of(piece, inner):
            row_copy(piece, index, False).wait_send()
            row_copy(piece, index, True).wait_recv()
            return inner

        lax.fori_loop(0, pieces, pieces_of, 0)
        return carry

    lax.fori_loop(0, count - 1, finish, 0)

    def close(piece, carry):
        for step in range(1, sharers):
            walk_copy(piece, step, False).wait_send()
        return carry

    lax.fori_loop(0, pieces, close, 0)


def two_parts(value):
    high = value.astype(jnp.bfloat16)
    return high, (value - high.astype(jnp.float32)).astype(jnp.bfloat16)


def exact(left, right, axis=1):
    left_high, left_low = two_parts(left)
    right_high, right_low = two_parts(right)
    return lax.dot_general(
        jnp.concatenate([left_high, left_low, left_high], axis=axis),
        jnp.concatenate([right_high, right_high, right_low], axis=0),
        (((axis,), (0,)), ((), ())), preferred_element_type=jnp.float32,
    )


def walker_phase(count, sharers, electrons, field_ref, whole_ref, out_ref,
                 send_sem, recv_sem, rows):
    me, walk = position(), lax.axis_index("walk")
    row_block = rows.shape[1]
    orbitals = field_ref.shape[1]
    others = partners(count, sharers)

    def swap(value, sign):
        return jnp.concatenate([-sign * value[:, LANES:], sign * value[:, :LANES]], axis=1)

    current = whole_ref[...].astype(jnp.float32)
    summed = current
    for order_index in range(1, TERMS + 1):
        rounded = current.astype(jnp.bfloat16)
        real = jnp.dot(field_ref[0], rounded, preferred_element_type=jnp.float32)
        imag = jnp.dot(field_ref[1], rounded, preferred_element_type=jnp.float32)
        current = (real + swap(imag, 1.0)) / order_index
        summed = summed + current
    squares = exact(summed, summed, 0) / orbitals
    gram_real = squares[:LANES, :LANES] + squares[LANES:, LANES:]
    gram_imag = squares[:LANES, LANES:] - squares[LANES:, :LANES]
    size = 2 * LANES
    identity = (
        lax.broadcasted_iota(jnp.int32, (size, size), 0)
        == lax.broadcasted_iota(jnp.int32, (size, size), 1)
    ).astype(jnp.float32)
    scale = jnp.sum(gram_real * identity[:LANES, :LANES]) / electrons
    top = jnp.concatenate([gram_real, gram_imag], axis=1)
    bottom = jnp.concatenate([-gram_imag, gram_real], axis=1)
    iterate = jnp.concatenate([top, bottom], axis=0) / scale
    step_of = 1.5 * identity - 0.5 * iterate
    root = step_of
    for sweep_index in range(1, NS_STEPS):
        iterate = exact(iterate, step_of)
        step_of = 1.5 * identity - 0.5 * exact(root, iterate)
        root = exact(step_of, root)
    normalized = exact(summed, root * lax.rsqrt(scale))
    rows[...] = normalized.reshape(count, row_block, size).astype(jnp.bfloat16)

    mine = walk * count + me
    for across, step, target in others:
        index = lax.rem(me + step, count)
        remote(rows.at[index], out_ref.at[mine], send_sem.at[across, step],
               recv_sem.at[across, step], target).start()
    out_ref[mine] = rows[me]
    for across, step, target in others:
        index = lax.rem(me + step, count)
        giver = lax.rem(walk + sharers - across, sharers) * count + lax.rem(
            me + count - step, count)
        remote(rows.at[index], out_ref.at[giver], send_sem.at[across, step],
               recv_sem.at[across, step], target).wait()


def step_kernel(count, sharers, electrons, columns_ref, inverse_ref, half_ref, samples_ref,
                vectors_ref, out_ref, columns, matrix, grid, half, theta, parts, arrived, coef, field, whole, spread,
                blocks, total, full, outgoing, incoming, finished, rows, half_sem, block_sem,
                theta_send, theta_recv, part_send, part_recv, coef_send, coef_recv,
                column_send, column_recv, walk_send, walk_recv, row_send, row_recv,
                out_send, out_recv):
    me = position()

    def first_half(step, carry):
        half_load(half_ref, half, half_sem, lax.rem(me + 1 + step, count)).start()
        return carry

    lax.fori_loop(0, count, first_half, 0)

    def first_blocks(step, carry):
        block_load(vectors_ref, blocks, block_sem, step).start()
        return carry

    lax.fori_loop(0, DEPTH - 1, first_blocks, 0)
    others = [target for _, _, target in partners(count, sharers)]
    barrier = greet(others)
    theta_phase(columns_ref, inverse_ref, theta, columns, matrix, grid)
    pl.semaphore_wait(barrier, len(others))
    bias_phase(count, sharers, half_ref, samples_ref, coef, half, theta, parts,
               arrived, half_sem, theta_send, theta_recv, part_send, part_recv, coef_send,
               coef_recv)
    column_phase(count, columns, whole, column_send, column_recv)
    field_phase(count, sharers, coef, columns, vectors_ref, field, whole, spread, blocks,
                total, full, outgoing, incoming, finished, block_sem, column_send, column_recv,
                walk_send, walk_recv, row_send, row_recv)
    walker_phase(count, sharers, electrons, field, whole, out_ref, out_send, out_recv, rows)


def body(walkers, correlation_inverse, half_vectors, field_vectors, samples, source):
    local_walkers = walkers.shape[0]
    vectors, row_block, orbitals = field_vectors.shape
    electrons = correlation_inverse.shape[2]
    flat = row_block * electrons
    count = lax.axis_size(("chol", "orb"))
    sharers = lax.axis_size("walk")
    width = vectors // count
    fits = (
        count == local_walkers and row_block % ROWS == 0 and local_walkers % HALF == 0
        and width % LANES == 0 and LANES % VECTORS == 0 and width == LANES
        and electrons <= LANES and orbitals % LANES == 0
        and flat % LANES == 0
        and (row_block // ROWS) * (orbitals // LANES) * (vectors // VECTORS) >= DEPTH
    )
    if not fits:
        return plain_body(
            walkers, correlation_inverse, half_vectors, field_vectors, samples, source
        )
    lines = sharers * 2 * local_walkers
    pieces = (row_block // ROWS) * (orbitals // LANES)
    chunks = vectors // VECTORS
    vmem, anywhere = pltpu.VMEM, pl.ANY
    dma = pltpu.SemaphoreType.DMA
    half_type, full_type = jnp.bfloat16, jnp.float32
    grid = walkers.reshape(local_walkers, 2, row_block, electrons)
    columns = jnp.pad(grid, ((0, 0), (0, 0), (0, 0), (0, LANES - electrons)))
    columns = columns.transpose(0, 2, 1, 3).reshape(local_walkers, row_block, 2 * LANES)
    moved = pl.pallas_call(
        functools.partial(step_kernel, count, sharers, electrons),
        out_shape=jax.ShapeDtypeStruct((sharers * local_walkers, row_block, 2 * LANES), half_type),
        in_specs=[
            pl.BlockSpec(memory_space=place) for place in (vmem, vmem, anywhere, vmem, anywhere)
        ],
        out_specs=pl.BlockSpec(memory_space=vmem),
        scratch_shapes=[
            vmem((local_walkers, row_block, 2 * LANES), half_type),
            vmem((2 * LANES, 2 * LANES), full_type),
            vmem((row_block, 2 * local_walkers, LANES), full_type),
            vmem((count, width, flat), half_type),
            vmem((sharers, 2 * local_walkers, flat), half_type),
            vmem((count, lines, width), full_type),
            vmem((count, lines, width), full_type),
            vmem((count, lines, width), half_type),
            vmem((2, orbitals, orbitals), half_type),
            vmem((orbitals, 2 * LANES), half_type),
            vmem((chunks, lines * HALF, VECTORS * HALF), half_type),
            vmem((DEPTH, VECTORS, ROWS, LANES), half_type),
            vmem((lines * HALF, 2 * LANES), full_type),
            vmem((pieces, sharers, local_walkers, 2, ROWS, LANES), full_type),
            vmem((pieces, sharers, local_walkers, 2, ROWS, LANES), half_type),
            vmem((pieces, sharers, local_walkers, 2, ROWS, LANES), half_type),
            vmem((pieces, local_walkers, 2, ROWS, LANES), half_type),
            vmem((count, row_block, 2 * LANES), half_type),
            dma((count,)), dma((DEPTH,)),
            dma((sharers,)), dma((sharers,)),
            dma((count,)), dma((count,)), dma((count,)), dma((count,)),
            dma((count,)), dma((count,)),
            dma((pieces, sharers)), dma((pieces, sharers)),
            dma((pieces, count)), dma((pieces, count)),
            dma((sharers, count)), dma((sharers, count)),
        ],
        compiler_params=pltpu.CompilerParams(
            collective_id=0, has_side_effects=True, vmem_limit_bytes=VMEM_LIMIT
        ),
    )(columns, correlation_inverse, half_vectors, samples, field_vectors)
    chosen = jnp.take(moved, source, axis=0).reshape(local_walkers, row_block, 2, LANES)
    chosen = chosen[..., :electrons].transpose(0, 2, 1, 3)
    return chosen.reshape(local_walkers, 2, flat).astype(walkers.dtype)


def solution(mesh):
    placed = (
        P(("groups", "walk"), None, ("chol", "orb")),
        P(("groups", "walk"), None, None, None),
        P(("groups", "walk"), ("chol", "orb")),
        P(("groups", "walk"), ("chol", "orb"), None),
        P("groups", "walk"),
        P(("groups", "walk")),
    )
    return jax.shard_map(
        body,
        mesh=mesh,
        in_specs=placed,
        out_specs=P(("groups", "walk"), None, ("chol", "orb")),
        check_vma=False,
    )
```

```python
import functools

import jax
import jax.numpy as jnp
from jax import lax
from jax.experimental import pallas as pl
from jax.experimental.pallas import tpu as pltpu
from jax.sharding import PartitionSpec as P

TERMS = 4
NS_STEPS = 2


def for_sending(shard):
    return jax.tree.map(lambda a: a.astype(jnp.bfloat16) if a.dtype == jnp.float32 else a, shard)


def complex_product(left_real, left_imag, right_real, right_imag, formula):
    first = jnp.einsum(formula, left_real, right_real, precision=lax.Precision.HIGHEST)
    second = jnp.einsum(formula, left_imag, right_imag, precision=lax.Precision.HIGHEST)
    third = jnp.einsum(formula, left_real, right_imag, precision=lax.Precision.HIGHEST)
    fourth = jnp.einsum(formula, left_imag, right_real, precision=lax.Precision.HIGHEST)
    return (first - second, third + fourth)


def normalizer(gram_real, gram_imag):
    electrons = gram_real.shape[-1]
    identity = jnp.eye(electrons, dtype=jnp.float32)
    scale_factor = jnp.trace(gram_real, axis1=1, axis2=2) / electrons
    iter_real = gram_real / scale_factor[:, None, None]
    iter_imag = gram_imag / scale_factor[:, None, None]
    root_real = jnp.broadcast_to(identity, gram_real.shape)
    root_imag = jnp.zeros_like(gram_real)
    for sweep_index in range(NS_STEPS):
        prod_real, prod_imag = complex_product(
            root_real, root_imag, iter_real, iter_imag, "wij,wjk->wik"
        )
        step_real = 1.5 * identity - 0.5 * prod_real
        step_imag = -0.5 * prod_imag
        iter_real, iter_imag = complex_product(
            iter_real, iter_imag, step_real, step_imag, "wij,wjk->wik"
        )
        root_real, root_imag = complex_product(
            step_real, step_imag, root_real, root_imag, "wij,wjk->wik"
        )
    inverse_root = lax.rsqrt(scale_factor)[:, None, None]
    return (root_real * inverse_root, root_imag * inverse_root)


def field_apply(field_block, values):
    next_real = jnp.einsum(
        "wab,wbn->wan", field_block[:, 0], values[:, 0], preferred_element_type=jnp.float32
    )
    next_real = next_real - jnp.einsum(
        "wab,wbn->wan", field_block[:, 1], values[:, 1], preferred_element_type=jnp.float32
    )
    next_imag = jnp.einsum(
        "wab,wbn->wan", field_block[:, 0], values[:, 1], preferred_element_type=jnp.float32
    )
    next_imag = next_imag + jnp.einsum(
        "wab,wbn->wan", field_block[:, 1], values[:, 0], preferred_element_type=jnp.float32
    )
    return jnp.stack([next_real, next_imag], 1)


def plain_body(walkers, correlation_inverse, half_vectors, field_vectors, samples, source):
    local_walkers = walkers.shape[0]
    row_block = field_vectors.shape[1]
    orbitals = field_vectors.shape[2]
    electrons = correlation_inverse.shape[2]
    grid = walkers.reshape(local_walkers, 2, row_block, electrons)
    theta_real, theta_imag = complex_product(
        grid[:, 0], grid[:, 1], correlation_inverse[:, 0], correlation_inverse[:, 1], "wmk,wkn->wmn"
    )
    theta = (
        jnp.stack([theta_real, theta_imag], 1)
        .reshape(local_walkers, 2, row_block * electrons)
        .astype(jnp.bfloat16)
    )
    all_theta = lax.all_gather(theta, "walk", axis=0, tiled=True)
    bias_part = jnp.einsum(
        "wcj,gj->wcg", all_theta, half_vectors, preferred_element_type=jnp.float32
    )
    bias = lax.psum(bias_part, ("chol", "orb"))
    coefficient = jnp.stack([bias[:, 1], samples - bias[:, 0]], 1).astype(jnp.bfloat16)
    field_part = jnp.einsum(
        "wcg,gab->wcab", coefficient, field_vectors, preferred_element_type=jnp.float32
    )
    field = lax.psum_scatter(field_part, "walk", scatter_dimension=0, tiled=True).astype(
        jnp.bfloat16
    )
    devices_rows = lax.axis_size(("chol", "orb"))
    sharers = devices_rows // local_walkers
    col_width = electrons // sharers
    parted = grid.reshape(local_walkers, 2, row_block, sharers, col_width)
    parted = parted.transpose(0, 3, 1, 2, 4).reshape(devices_rows, 2, row_block, col_width)
    columns = lax.all_to_all(
        parted.astype(jnp.bfloat16), ("chol", "orb"), split_axis=0, concat_axis=2, tiled=True
    ).astype(parted.dtype)
    spread = jnp.broadcast_to(field[:, None], (local_walkers, sharers, 2, row_block, orbitals))
    spread = spread.reshape(devices_rows, 2, row_block, orbitals)
    whole_field = lax.all_to_all(spread, ("chol", "orb"), split_axis=0, concat_axis=2, tiled=True)
    current = columns
    col_summed = columns
    for order_index in range(1, TERMS + 1):
        current = field_apply(whole_field, current.astype(jnp.bfloat16)) / order_index
        col_summed = col_summed + current
    returned = lax.all_to_all(
        col_summed.astype(jnp.bfloat16), ("chol", "orb"), split_axis=2, concat_axis=0, tiled=True
    ).astype(col_summed.dtype)
    returned = returned.reshape(local_walkers, sharers, 2, row_block, col_width)
    summed = returned.transpose(0, 2, 3, 1, 4).reshape(local_walkers, 2, row_block, electrons)
    whole = lax.all_gather(summed.astype(jnp.bfloat16), ("chol", "orb"), axis=2, tiled=True).astype(
        summed.dtype
    )
    gram_real, gram_imag = complex_product(
        whole[:, 0], -whole[:, 1], whole[:, 0], whole[:, 1], "wmi,wmj->wij"
    )
    gram_real = gram_real / orbitals
    gram_imag = gram_imag / orbitals
    root_real, root_imag = normalizer(gram_real, gram_imag)
    norm_real, norm_imag = complex_product(
        summed[:, 0], summed[:, 1], root_real, root_imag, "wmk,wkn->wmn"
    )
    normalized = jnp.stack([norm_real, norm_imag], 1).reshape(
        local_walkers, 2, row_block * electrons
    )
    moved = lax.all_gather(for_sending(normalized), "walk", axis=0, tiled=True).astype(
        normalized.dtype
    )
    return jnp.take(moved, source, axis=0)


MESH = pl.DeviceIdType.MESH
LANES = 128
HALF = 8
ROWS = 16
VECTORS = 128
DEPTH = 16
VMEM_LIMIT = 60 * 1024 * 1024


def owner_id(index):
    orbs = lax.axis_size("orb")
    return {"chol": index // orbs, "orb": lax.rem(index, orbs)}


def position():
    return lax.axis_index("chol") * lax.axis_size("orb") + lax.axis_index("orb")


def greet(devices):
    barrier = pltpu.get_barrier_semaphore()
    for device in devices:
        pl.semaphore_signal(barrier, inc=1, device_id=device, device_id_type=MESH)
    return barrier


def partners(count, sharers):
    me, walk = position(), lax.axis_index("walk")
    others = []
    for across in range(sharers):
        for step in range(count):
            if across + step > 0:
                target = owner_id(lax.rem(me + step, count))
                target["walk"] = lax.rem(walk + across, sharers)
                others.append((across, step, target))
    return others


def remote(source, target, send, recv, device):
    return pltpu.make_async_remote_copy(
        src_ref=source, dst_ref=target, send_sem=send, recv_sem=recv,
        device_id=device, device_id_type=MESH,
    )


def theta_phase(columns_ref, inverse_ref, theta, columns, matrices, grid):
    walk = lax.axis_index("walk")
    local, row_block = columns_ref.shape[0], columns_ref.shape[1]
    electrons = inverse_ref.shape[2]
    size = 2 * LANES
    matrices[...] = jnp.zeros_like(matrices)
    for walker in range(local):
        matrix = matrices.at[walker % 2]
        real_parts = two_parts(inverse_ref[walker, 0])
        imag_parts = two_parts(inverse_ref[walker, 1])
        for place, part in enumerate((0, 0, 1)):
            first, second = place * size, place * size + LANES
            matrix[first:first + electrons, :electrons] = real_parts[part]
            matrix[first:first + electrons, LANES:LANES + electrons] = imag_parts[part]
            matrix[second:second + electrons, :electrons] = -imag_parts[part]
            matrix[second:second + electrons, LANES:LANES + electrons] = real_parts[part]
        high, low = two_parts(columns_ref[walker])
        columns[walker] = high
        rotated = jnp.dot(jnp.concatenate([high, low, high], axis=1), matrix[...],
                          preferred_element_type=jnp.float32)
        grid[:, walker, :] = rotated[:, :LANES]
        grid[:, local + walker, :] = rotated[:, LANES:]
    lane = lax.broadcasted_iota(jnp.int32, (2 * local, LANES), 1)
    for tile in range(row_block * electrons // LANES):
        start = tile * LANES
        value = None
        for row in range(start // electrons, (start + LANES - 1) // electrons + 1):
            moved = pltpu.roll(grid[row], row * electrons % LANES, 1)
            value = moved if value is None else jnp.where(
                lane < row * electrons - start, value, moved)
        theta[walk, :, start:start + LANES] = value.astype(jnp.bfloat16)


def half_load(half_ref, half, load_sem, index):
    width = half.shape[1]
    return pltpu.make_async_copy(
        half_ref.at[pl.ds(pl.multiple_of(index * width, width), width), :],
        half.at[index], load_sem.at[index],
    )


def block_load(vectors_ref, blocks, load_sem, step):
    chunks = vectors_ref.shape[0] // VECTORS
    group, chunk = step // chunks, lax.rem(step, chunks)
    slot = lax.rem(step, DEPTH)
    return pltpu.make_async_copy(
        vectors_ref.at[pl.ds(pl.multiple_of(chunk * VECTORS, VECTORS), VECTORS),
                       pl.ds(pl.multiple_of(group * ROWS, ROWS), ROWS), :],
        blocks.at[slot], load_sem.at[slot],
    )


def column_phase(count, columns_ref, whole_ref, column_send, column_recv):
    me = position()
    row_block = columns_ref.shape[1]
    here = pl.ds(pl.multiple_of(me * row_block, ROWS), row_block)

    def send_columns(step, carry):
        index = lax.rem(me + 1 + step, count)
        remote(columns_ref.at[index], whole_ref.at[here, :], column_send.at[index],
               column_recv.at[me], owner_id(index)).start()
        return carry

    lax.fori_loop(0, count - 1, send_columns, 0)
    whole_ref[here, :] = columns_ref[me]


def bias_phase(count, sharers, half_ref, samples_ref, coef_ref,
                half, theta, parts, arrived, load_sem, theta_send, theta_recv,
                part_send, part_recv, coef_send, coef_recv):
    me, walk = position(), lax.axis_index("walk")
    width = half.shape[1]
    local = theta.shape[1] // 2

    def load(index):
        return half_load(half_ref, half, load_sem, index)

    sends = []
    for step in range(1, sharers):
        other = lax.rem(walk + step, sharers)
        sends.append(remote(theta.at[walk], theta.at[walk], theta_send.at[step],
                            theta_recv.at[walk], {"walk": other}))
        sends[-1].start()
    for step in range(1, sharers):
        other = lax.rem(walk + step, sharers)
        remote(theta.at[walk], theta.at[other], theta_send.at[step],
               theta_recv.at[other], {"walk": other}).wait_recv()

    def part_copy(index):
        return remote(parts.at[index], arrived.at[me], part_send.at[index],
                      part_recv.at[me], owner_id(index))

    def one(step, carry):
        pair = lax.rem(me // 2 + 1 + step, count // 2)
        for side in range(2):
            load(pair * 2 + side).wait()
        product = lax.dot_general(
            theta[...].reshape(sharers * 2 * local, theta.shape[2]),
            half[pl.ds(pair * 2, 2)].reshape(2 * width, theta.shape[2]),
            (((1,), (1,)), ((), ())), preferred_element_type=jnp.float32,
        )
        for side in range(2):
            index = pair * 2 + side
            value = product[:, side * width:(side + 1) * width]

            @pl.when(index == me)
            def _():
                arrived[me] = value

            @pl.when(index != me)
            def _():
                parts[index] = value
                part_copy(index).start()

        return carry

    lax.fori_loop(0, count // 2, one, 0)

    def take(step, carry):
        index = lax.rem(me + 1 + step, count)
        remote(parts.at[index], arrived.at[index], part_send.at[index],
               part_recv.at[index], owner_id(index)).wait_recv()
        return carry

    lax.fori_loop(0, count - 1, take, 0)
    bias = jnp.sum(arrived[...], axis=0).reshape(sharers, 2, local, width)
    chosen = samples_ref[:, pl.ds(pl.multiple_of(me * width, width), width)]
    chosen = chosen.reshape(sharers, local, width)
    pair = jnp.stack([bias[:, 1], chosen - bias[:, 0]], 1)
    coef_ref[me] = pair.reshape(sharers * 2 * local, width).astype(jnp.bfloat16)

    def spread(step, carry):
        index = lax.rem(me + 1 + step, count)
        remote(coef_ref.at[me], coef_ref.at[me], coef_send.at[index],
               coef_recv.at[me], owner_id(index)).start()
        return carry

    lax.fori_loop(0, count - 1, spread, 0)

    def finish(step, carry):
        index = lax.rem(me + 1 + step, count)
        part_copy(index).wait_send()
        remote(coef_ref.at[me], coef_ref.at[index], coef_send.at[index],
               coef_recv.at[index], owner_id(index)).wait()
        return carry

    lax.fori_loop(0, count - 1, finish, 0)
    for send in sends:
        send.wait_send()


def field_phase(count, sharers, coef_ref, columns_ref, vectors_ref, field_ref, whole_ref,
                 spread, blocks, total, full, outgoing, incoming, finished,
                 load_sem, column_send, column_recv, walk_send, walk_recv,
                 row_send, row_recv):
    me, walk = position(), lax.axis_index("walk")
    local = columns_ref.shape[0]
    row_block = columns_ref.shape[1]
    orbitals = vectors_ref.shape[2]
    chunks = vectors_ref.shape[0] // VECTORS
    groups = row_block // ROWS
    lines = coef_ref.shape[1]
    per_block = coef_ref.shape[2] // VECTORS
    depth = VECTORS * HALF

    def load(step):
        return block_load(vectors_ref, blocks, load_sem, step)

    vector_at = lax.broadcasted_iota(jnp.int32, (LANES, depth), 0)
    place = lax.broadcasted_iota(jnp.int32, (LANES, depth), 1)
    row_at = lax.broadcasted_iota(jnp.int32, (HALF, depth), 0)
    row_place = lax.broadcasted_iota(jnp.int32, (HALF, depth), 1)
    diagonal = (lax.rem(row_place, HALF) == row_at).astype(jnp.float32)

    for part in range(per_block):
        picks = (vector_at == place // HALF + part * VECTORS).astype(jnp.bfloat16)

        def widen(block, carry):
            repeated = jnp.dot(coef_ref[block], picks, preferred_element_type=jnp.float32)
            wide = repeated[:, None, :] * diagonal[None]
            spread[block * per_block + part] = wide.reshape(lines * HALF, depth).astype(
                jnp.bfloat16
            )
            return carry

        lax.fori_loop(0, coef_ref.shape[0], widen, 0)

    def walk_copy(group, step, arriving):
        other = lax.rem(walk + step, sharers) if not arriving else lax.rem(
            walk + sharers - step, sharers)
        return remote(outgoing.at[group, other], incoming.at[group, other if arriving else walk],
                      walk_send.at[group, other], walk_recv.at[group, other if arriving else walk],
                      {"walk": other})

    def row_copy(group, index, arriving):
        giver = index if arriving else me
        at = pl.ds(pl.multiple_of(giver * row_block + group * ROWS, ROWS), ROWS)
        return remote(finished.at[group, index], field_ref.at[:, at, :],
                      row_send.at[group, index], row_recv.at[group, giver], owner_id(index))

    def deliver(group):
        result = full[group, walk]
        for step in range(1, sharers):
            walk_copy(group, step, True).wait_recv()
            other = lax.rem(walk + sharers - step, sharers)
            result = result + incoming[group, other].astype(jnp.float32)
        finished[group] = result.astype(jnp.bfloat16)

        def send_rows(step, carry):
            row_copy(group, lax.rem(me + 1 + step, count), False).start()
            return carry

        lax.fori_loop(0, count - 1, send_rows, 0)
        field_ref[:, pl.ds(pl.multiple_of(me * row_block + group * ROWS, ROWS), ROWS), :] = (
            finished[group, me]
        )

    for group in range(groups):
        total[...] = jnp.zeros_like(total)

        def add(chunk, carry):
            step = group * chunks + chunk

            @pl.when(step + DEPTH - 1 < groups * chunks)
            def _():
                load(step + DEPTH - 1).start()

            load(step).wait()
            slot = lax.rem(step, DEPTH)
            upper = blocks[slot, :, :HALF, :].reshape(depth, orbitals)
            lower = blocks[slot, :, HALF:, :].reshape(depth, orbitals)
            total[...] += jnp.dot(
                spread[chunk], jnp.concatenate([upper, lower], axis=1),
                preferred_element_type=jnp.float32,
            )
            return carry

        lax.fori_loop(0, chunks, add, 0)
        result = total[...].reshape(sharers, 2, local, HALF, 2 * orbitals)
        result = jnp.concatenate([result[..., :orbitals], result[..., orbitals:]], axis=3)
        for part in range(2):
            full[group, :, :, part] = result[:, part]
            outgoing[group, :, :, part] = result[:, part].astype(jnp.bfloat16)
        for step in range(1, sharers):
            walk_copy(group, step, False).start()
        if group > 0:
            deliver(group - 1)
    deliver(groups - 1)

    def finish(step, carry):
        index = lax.rem(me + 1 + step, count)
        there = pl.ds(pl.multiple_of(index * row_block, ROWS), row_block)
        remote(columns_ref.at[index], whole_ref.at[there, :], column_send.at[index],
               column_recv.at[index], owner_id(index)).wait()
        for group in range(groups):
            row_copy(group, index, False).wait_send()
            row_copy(group, index, True).wait_recv()
        return carry

    lax.fori_loop(0, count - 1, finish, 0)
    for group in range(groups):
        for step in range(1, sharers):
            walk_copy(group, step, False).wait_send()


def two_parts(value):
    high = value.astype(jnp.bfloat16)
    return high, (value - high.astype(jnp.float32)).astype(jnp.bfloat16)


def exact(left, right, axis=1):
    left_high, left_low = two_parts(left)
    right_high, right_low = two_parts(right)
    return lax.dot_general(
        jnp.concatenate([left_high, left_low, left_high], axis=axis),
        jnp.concatenate([right_high, right_high, right_low], axis=0),
        (((axis,), (0,)), ((), ())), preferred_element_type=jnp.float32,
    )


def walker_phase(count, sharers, electrons, field_ref, whole_ref, out_ref,
                 send_sem, recv_sem, rows):
    me, walk = position(), lax.axis_index("walk")
    row_block = rows.shape[1]
    orbitals = field_ref.shape[1]
    others = partners(count, sharers)

    def swap(value, sign):
        return jnp.concatenate([-sign * value[:, LANES:], sign * value[:, :LANES]], axis=1)

    current = whole_ref[...].astype(jnp.float32)
    summed = current
    for order_index in range(1, TERMS + 1):
        rounded = current.astype(jnp.bfloat16)
        real = jnp.dot(field_ref[0], rounded, preferred_element_type=jnp.float32)
        imag = jnp.dot(field_ref[1], rounded, preferred_element_type=jnp.float32)
        current = (real + swap(imag, 1.0)) / order_index
        summed = summed + current
    squares = exact(summed, summed, 0) / orbitals
    gram_real = squares[:LANES, :LANES] + squares[LANES:, LANES:]
    gram_imag = squares[:LANES, LANES:] - squares[LANES:, :LANES]
    size = 2 * LANES
    identity = (
        lax.broadcasted_iota(jnp.int32, (size, size), 0)
        == lax.broadcasted_iota(jnp.int32, (size, size), 1)
    ).astype(jnp.float32)
    scale = jnp.sum(gram_real * identity[:LANES, :LANES]) / electrons
    top = jnp.concatenate([gram_real, gram_imag], axis=1)
    bottom = jnp.concatenate([-gram_imag, gram_real], axis=1)
    iterate = jnp.concatenate([top, bottom], axis=0) / scale
    step_of = 1.5 * identity - 0.5 * iterate
    root = step_of
    for sweep_index in range(1, NS_STEPS):
        iterate = exact(iterate, step_of)
        step_of = 1.5 * identity - 0.5 * exact(root, iterate)
        root = exact(step_of, root)
    normalized = exact(summed, root * lax.rsqrt(scale))
    rows[...] = normalized.reshape(count, row_block, size).astype(jnp.bfloat16)

    mine = walk * count + me
    for across, step, target in others:
        index = lax.rem(me + step, count)
        remote(rows.at[index], out_ref.at[mine], send_sem.at[across, step],
               recv_sem.at[across, step], target).start()
    out_ref[mine] = rows[me]
    for across, step, target in others:
        index = lax.rem(me + step, count)
        giver = lax.rem(walk + sharers - across, sharers) * count + lax.rem(
            me + count - step, count)
        remote(rows.at[index], out_ref.at[giver], send_sem.at[across, step],
               recv_sem.at[across, step], target).wait()


def step_kernel(count, sharers, electrons, columns_ref, inverse_ref, half_ref, samples_ref,
                vectors_ref, out_ref, columns, matrices, grid, half, theta, parts, arrived, coef, field, whole, spread,
                blocks, total, full, outgoing, incoming, finished, rows, half_sem, block_sem,
                theta_send, theta_recv, part_send, part_recv, coef_send, coef_recv,
                column_send, column_recv, walk_send, walk_recv, row_send, row_recv,
                out_send, out_recv):
    me = position()

    def first_half(step, carry):
        half_load(half_ref, half, half_sem, lax.rem((me // 2) * 2 + 2 + step, count)).start()
        return carry

    lax.fori_loop(0, count, first_half, 0)

    def first_blocks(step, carry):
        block_load(vectors_ref, blocks, block_sem, step).start()
        return carry

    lax.fori_loop(0, DEPTH - 1, first_blocks, 0)
    others = [target for _, _, target in partners(count, sharers)]
    barrier = greet(others)
    theta_phase(columns_ref, inverse_ref, theta, columns, matrices, grid)
    pl.semaphore_wait(barrier, len(others))
    bias_phase(count, sharers, half_ref, samples_ref, coef, half, theta, parts,
               arrived, half_sem, theta_send, theta_recv, part_send, part_recv, coef_send,
               coef_recv)
    column_phase(count, columns, whole, column_send, column_recv)
    field_phase(count, sharers, coef, columns, vectors_ref, field, whole, spread, blocks,
                total, full, outgoing, incoming, finished, block_sem, column_send, column_recv,
                walk_send, walk_recv, row_send, row_recv)
    walker_phase(count, sharers, electrons, field, whole, out_ref, out_send, out_recv, rows)


def body(walkers, correlation_inverse, half_vectors, field_vectors, samples, source):
    local_walkers = walkers.shape[0]
    vectors, row_block, orbitals = field_vectors.shape
    electrons = correlation_inverse.shape[2]
    flat = row_block * electrons
    count = lax.axis_size(("chol", "orb"))
    sharers = lax.axis_size("walk")
    width = vectors // count
    fits = (
        count == local_walkers and row_block % ROWS == 0 and local_walkers % HALF == 0
        and width % LANES == 0 and LANES % VECTORS == 0 and width == LANES
        and electrons <= LANES and orbitals % LANES == 0
        and flat % LANES == 0 and count % 2 == 0 and electrons % ROWS == 0
        and (row_block // ROWS) * (vectors // VECTORS) >= DEPTH
    )
    if not fits:
        return plain_body(
            walkers, correlation_inverse, half_vectors, field_vectors, samples, source
        )
    lines = sharers * 2 * local_walkers
    groups = row_block // ROWS
    chunks = vectors // VECTORS
    vmem, anywhere = pltpu.VMEM, pl.ANY
    dma = pltpu.SemaphoreType.DMA
    half_type, full_type = jnp.bfloat16, jnp.float32
    grid = walkers.reshape(local_walkers, 2, row_block, electrons)
    columns = jnp.pad(grid, ((0, 0), (0, 0), (0, 0), (0, LANES - electrons)))
    columns = columns.transpose(0, 2, 1, 3).reshape(local_walkers, row_block, 2 * LANES)
    moved = pl.pallas_call(
        functools.partial(step_kernel, count, sharers, electrons),
        out_shape=jax.ShapeDtypeStruct((sharers * local_walkers, row_block, 2 * LANES), half_type),
        in_specs=[
            pl.BlockSpec(memory_space=place) for place in (vmem, vmem, anywhere, vmem, anywhere)
        ],
        out_specs=pl.BlockSpec(memory_space=vmem),
        scratch_shapes=[
            vmem((local_walkers, row_block, 2 * LANES), half_type),
            vmem((2, 6 * LANES, 2 * LANES), half_type),
            vmem((row_block, 2 * local_walkers, LANES), full_type),
            vmem((count, width, flat), half_type),
            vmem((sharers, 2 * local_walkers, flat), half_type),
            vmem((count, lines, width), full_type),
            vmem((count, lines, width), full_type),
            vmem((count, lines, width), half_type),
            vmem((2, orbitals, orbitals), half_type),
            vmem((orbitals, 2 * LANES), half_type),
            vmem((chunks, lines * HALF, VECTORS * HALF), half_type),
            vmem((DEPTH, VECTORS, ROWS, orbitals), half_type),
            vmem((lines * HALF, 2 * orbitals), full_type),
            vmem((groups, sharers, local_walkers, 2, ROWS, orbitals), full_type),
            vmem((groups, sharers, local_walkers, 2, ROWS, orbitals), half_type),
            vmem((groups, sharers, local_walkers, 2, ROWS, orbitals), half_type),
            vmem((groups, local_walkers, 2, ROWS, orbitals), half_type),
            vmem((count, row_block, 2 * LANES), half_type),
            dma((count,)), dma((DEPTH,)),
            dma((sharers,)), dma((sharers,)),
            dma((count,)), dma((count,)), dma((count,)), dma((count,)),
            dma((count,)), dma((count,)),
            dma((groups, sharers)), dma((groups, sharers)),
            dma((groups, count)), dma((groups, count)),
            dma((sharers, count)), dma((sharers, count)),
        ],
        compiler_params=pltpu.CompilerParams(
            collective_id=0, has_side_effects=True, vmem_limit_bytes=VMEM_LIMIT
        ),
    )(columns, correlation_inverse, half_vectors, samples, field_vectors)
    chosen = jnp.take(moved, source, axis=0).reshape(local_walkers, row_block, 2, LANES)
    chosen = chosen[..., :electrons].transpose(0, 2, 1, 3)
    return chosen.reshape(local_walkers, 2, flat).astype(walkers.dtype)


def solution(mesh):
    placed = (
        P(("groups", "walk"), None, ("chol", "orb")),
        P(("groups", "walk"), None, None, None),
        P(("groups", "walk"), ("chol", "orb")),
        P(("groups", "walk"), ("chol", "orb"), None),
        P("groups", "walk"),
        P(("groups", "walk")),
    )
    return jax.shard_map(
        body,
        mesh=mesh,
        in_specs=placed,
        out_specs=P(("groups", "walk"), None, ("chol", "orb")),
        check_vma=False,
    )
```

```python
import functools

import jax
import jax.numpy as jnp
from jax import lax
from jax.experimental import pallas as pl
from jax.experimental.pallas import tpu as pltpu
from jax.sharding import PartitionSpec as P

TERMS = 4
NS_STEPS = 2


def for_sending(shard):
    return jax.tree.map(lambda a: a.astype(jnp.bfloat16) if a.dtype == jnp.float32 else a, shard)


def complex_product(left_real, left_imag, right_real, right_imag, formula):
    first = jnp.einsum(formula, left_real, right_real, precision=lax.Precision.HIGHEST)
    second = jnp.einsum(formula, left_imag, right_imag, precision=lax.Precision.HIGHEST)
    third = jnp.einsum(formula, left_real, right_imag, precision=lax.Precision.HIGHEST)
    fourth = jnp.einsum(formula, left_imag, right_real, precision=lax.Precision.HIGHEST)
    return (first - second, third + fourth)


def normalizer(gram_real, gram_imag):
    electrons = gram_real.shape[-1]
    identity = jnp.eye(electrons, dtype=jnp.float32)
    scale_factor = jnp.trace(gram_real, axis1=1, axis2=2) / electrons
    iter_real = gram_real / scale_factor[:, None, None]
    iter_imag = gram_imag / scale_factor[:, None, None]
    root_real = jnp.broadcast_to(identity, gram_real.shape)
    root_imag = jnp.zeros_like(gram_real)
    for sweep_index in range(NS_STEPS):
        prod_real, prod_imag = complex_product(
            root_real, root_imag, iter_real, iter_imag, "wij,wjk->wik"
        )
        step_real = 1.5 * identity - 0.5 * prod_real
        step_imag = -0.5 * prod_imag
        iter_real, iter_imag = complex_product(
            iter_real, iter_imag, step_real, step_imag, "wij,wjk->wik"
        )
        root_real, root_imag = complex_product(
            step_real, step_imag, root_real, root_imag, "wij,wjk->wik"
        )
    inverse_root = lax.rsqrt(scale_factor)[:, None, None]
    return (root_real * inverse_root, root_imag * inverse_root)


def field_apply(field_block, values):
    next_real = jnp.einsum(
        "wab,wbn->wan", field_block[:, 0], values[:, 0], preferred_element_type=jnp.float32
    )
    next_real = next_real - jnp.einsum(
        "wab,wbn->wan", field_block[:, 1], values[:, 1], preferred_element_type=jnp.float32
    )
    next_imag = jnp.einsum(
        "wab,wbn->wan", field_block[:, 0], values[:, 1], preferred_element_type=jnp.float32
    )
    next_imag = next_imag + jnp.einsum(
        "wab,wbn->wan", field_block[:, 1], values[:, 0], preferred_element_type=jnp.float32
    )
    return jnp.stack([next_real, next_imag], 1)


def plain_body(walkers, correlation_inverse, half_vectors, field_vectors, samples, source):
    local_walkers = walkers.shape[0]
    row_block = field_vectors.shape[1]
    orbitals = field_vectors.shape[2]
    electrons = correlation_inverse.shape[2]
    grid = walkers.reshape(local_walkers, 2, row_block, electrons)
    theta_real, theta_imag = complex_product(
        grid[:, 0], grid[:, 1], correlation_inverse[:, 0], correlation_inverse[:, 1], "wmk,wkn->wmn"
    )
    theta = (
        jnp.stack([theta_real, theta_imag], 1)
        .reshape(local_walkers, 2, row_block * electrons)
        .astype(jnp.bfloat16)
    )
    all_theta = lax.all_gather(theta, "walk", axis=0, tiled=True)
    bias_part = jnp.einsum(
        "wcj,gj->wcg", all_theta, half_vectors, preferred_element_type=jnp.float32
    )
    bias = lax.psum(bias_part, ("chol", "orb"))
    coefficient = jnp.stack([bias[:, 1], samples - bias[:, 0]], 1).astype(jnp.bfloat16)
    field_part = jnp.einsum(
        "wcg,gab->wcab", coefficient, field_vectors, preferred_element_type=jnp.float32
    )
    field = lax.psum_scatter(field_part, "walk", scatter_dimension=0, tiled=True).astype(
        jnp.bfloat16
    )
    devices_rows = lax.axis_size(("chol", "orb"))
    sharers = devices_rows // local_walkers
    col_width = electrons // sharers
    parted = grid.reshape(local_walkers, 2, row_block, sharers, col_width)
    parted = parted.transpose(0, 3, 1, 2, 4).reshape(devices_rows, 2, row_block, col_width)
    columns = lax.all_to_all(
        parted.astype(jnp.bfloat16), ("chol", "orb"), split_axis=0, concat_axis=2, tiled=True
    ).astype(parted.dtype)
    spread = jnp.broadcast_to(field[:, None], (local_walkers, sharers, 2, row_block, orbitals))
    spread = spread.reshape(devices_rows, 2, row_block, orbitals)
    whole_field = lax.all_to_all(spread, ("chol", "orb"), split_axis=0, concat_axis=2, tiled=True)
    current = columns
    col_summed = columns
    for order_index in range(1, TERMS + 1):
        current = field_apply(whole_field, current.astype(jnp.bfloat16)) / order_index
        col_summed = col_summed + current
    returned = lax.all_to_all(
        col_summed.astype(jnp.bfloat16), ("chol", "orb"), split_axis=2, concat_axis=0, tiled=True
    ).astype(col_summed.dtype)
    returned = returned.reshape(local_walkers, sharers, 2, row_block, col_width)
    summed = returned.transpose(0, 2, 3, 1, 4).reshape(local_walkers, 2, row_block, electrons)
    whole = lax.all_gather(summed.astype(jnp.bfloat16), ("chol", "orb"), axis=2, tiled=True).astype(
        summed.dtype
    )
    gram_real, gram_imag = complex_product(
        whole[:, 0], -whole[:, 1], whole[:, 0], whole[:, 1], "wmi,wmj->wij"
    )
    gram_real = gram_real / orbitals
    gram_imag = gram_imag / orbitals
    root_real, root_imag = normalizer(gram_real, gram_imag)
    norm_real, norm_imag = complex_product(
        summed[:, 0], summed[:, 1], root_real, root_imag, "wmk,wkn->wmn"
    )
    normalized = jnp.stack([norm_real, norm_imag], 1).reshape(
        local_walkers, 2, row_block * electrons
    )
    moved = lax.all_gather(for_sending(normalized), "walk", axis=0, tiled=True).astype(
        normalized.dtype
    )
    return jnp.take(moved, source, axis=0)


MESH = pl.DeviceIdType.MESH
LANES = 128
HALF = 8
ROWS = 16
VECTORS = 128
DEPTH = 16
VMEM_LIMIT = 60 * 1024 * 1024


def owner_id(index):
    orbs = lax.axis_size("orb")
    return {"chol": index // orbs, "orb": lax.rem(index, orbs)}


def position():
    return lax.axis_index("chol") * lax.axis_size("orb") + lax.axis_index("orb")


def greet(devices):
    barrier = pltpu.get_barrier_semaphore()
    for device in devices:
        pl.semaphore_signal(barrier, inc=1, device_id=device, device_id_type=MESH)
    return barrier


def partners(count, sharers):
    me, walk = position(), lax.axis_index("walk")
    others = []
    for across in range(sharers):
        for step in range(count):
            if across + step > 0:
                target = owner_id(lax.rem(me + step, count))
                target["walk"] = lax.rem(walk + across, sharers)
                others.append((across, step, target))
    return others


def remote(source, target, send, recv, device):
    return pltpu.make_async_remote_copy(
        src_ref=source, dst_ref=target, send_sem=send, recv_sem=recv,
        device_id=device, device_id_type=MESH,
    )


def to_rows(flat_ref, grid, electrons):
    lane = lax.broadcasted_iota(jnp.int32, (flat_ref.shape[0], LANES), 1)
    for row in range(grid.shape[0]):
        start, shift = row * electrons // LANES * LANES, row * electrons % LANES
        back = (LANES - shift) % LANES
        value = pltpu.roll(flat_ref[:, start:start + LANES], back, 1)
        if shift + electrons > LANES:
            after = pltpu.roll(flat_ref[:, start + LANES:start + 2 * LANES], back, 1)
            value = jnp.where(lane < LANES - shift, value, after)
        grid[row] = jnp.where(lane < electrons, value, 0.0)


def to_flat(grid, electrons):
    lane = lax.broadcasted_iota(jnp.int32, (grid.shape[1], LANES), 1)
    for tile in range(grid.shape[0] * electrons // LANES):
        start = tile * LANES
        value = None
        for row in range(start // electrons, (start + LANES - 1) // electrons + 1):
            moved = pltpu.roll(grid[row], row * electrons % LANES, 1)
            value = moved if value is None else jnp.where(
                lane < row * electrons - start, value, moved)
        yield start, value


def theta_phase(walkers_ref, inverse_ref, theta, columns, matrices, rows_in, grid):
    walk = lax.axis_index("walk")
    local = inverse_ref.shape[0]
    electrons = inverse_ref.shape[2]
    to_rows(walkers_ref, rows_in, electrons)
    size = 2 * LANES
    matrices[...] = jnp.zeros_like(matrices)
    for walker in range(local):
        matrix = matrices.at[walker % 2]
        real_parts = two_parts(inverse_ref[walker, 0])
        imag_parts = two_parts(inverse_ref[walker, 1])
        for place, part in enumerate((0, 0, 1)):
            first, second = place * size, place * size + LANES
            matrix[first:first + electrons, :electrons] = real_parts[part]
            matrix[first:first + electrons, LANES:LANES + electrons] = imag_parts[part]
            matrix[second:second + electrons, :electrons] = -imag_parts[part]
            matrix[second:second + electrons, LANES:LANES + electrons] = real_parts[part]
        pair = [rows_in[:, 2 * walker + side, :] for side in range(2)]
        high, low = two_parts(jnp.concatenate(pair, axis=1))
        columns[walker] = high
        rotated = jnp.dot(jnp.concatenate([high, low, high], axis=1), matrix[...],
                          preferred_element_type=jnp.float32)
        grid[:, walker, :] = rotated[:, :LANES]
        grid[:, local + walker, :] = rotated[:, LANES:]
    for start, value in to_flat(grid, electrons):
        theta[walk, :, start:start + LANES] = value.astype(jnp.bfloat16)


def half_load(half_ref, half, load_sem, index):
    width = half.shape[1]
    return pltpu.make_async_copy(
        half_ref.at[pl.ds(pl.multiple_of(index * width, width), width), :],
        half.at[index], load_sem.at[index],
    )


def block_load(vectors_ref, blocks, load_sem, step):
    chunks = vectors_ref.shape[0] // VECTORS
    group, chunk = step // chunks, lax.rem(step, chunks)
    slot = lax.rem(step, DEPTH)
    return pltpu.make_async_copy(
        vectors_ref.at[pl.ds(pl.multiple_of(chunk * VECTORS, VECTORS), VECTORS),
                       pl.ds(pl.multiple_of(group * ROWS, ROWS), ROWS), :],
        blocks.at[slot], load_sem.at[slot],
    )


def column_phase(count, columns_ref, whole_ref, column_send, column_recv):
    me = position()
    row_block = columns_ref.shape[1]
    here = pl.ds(pl.multiple_of(me * row_block, ROWS), row_block)

    def send_columns(step, carry):
        index = lax.rem(me + 1 + step, count)
        remote(columns_ref.at[index], whole_ref.at[here, :], column_send.at[index],
               column_recv.at[me], owner_id(index)).start()
        return carry

    lax.fori_loop(0, count - 1, send_columns, 0)
    whole_ref[here, :] = columns_ref[me]


def bias_phase(count, sharers, half_ref, samples_ref, coef_ref,
                half, theta, parts, arrived, load_sem, theta_send, theta_recv,
                part_send, part_recv, coef_send, coef_recv):
    me, walk = position(), lax.axis_index("walk")
    width = half.shape[1]
    local = theta.shape[1] // 2

    def load(index):
        return half_load(half_ref, half, load_sem, index)

    sends = []
    for step in range(1, sharers):
        other = lax.rem(walk + step, sharers)
        sends.append(remote(theta.at[walk], theta.at[walk], theta_send.at[step],
                            theta_recv.at[walk], {"walk": other}))
        sends[-1].start()
    for step in range(1, sharers):
        other = lax.rem(walk + step, sharers)
        remote(theta.at[walk], theta.at[other], theta_send.at[step],
               theta_recv.at[other], {"walk": other}).wait_recv()

    def part_copy(index):
        return remote(parts.at[index], arrived.at[me], part_send.at[index],
                      part_recv.at[me], owner_id(index))

    def one(step, carry):
        pair = lax.rem(me // 2 + 1 + step, count // 2)
        for side in range(2):
            load(pair * 2 + side).wait()
        product = lax.dot_general(
            theta[...].reshape(sharers * 2 * local, theta.shape[2]),
            half[pl.ds(pair * 2, 2)].reshape(2 * width, theta.shape[2]),
            (((1,), (1,)), ((), ())), preferred_element_type=jnp.float32,
        )
        for side in range(2):
            index = pair * 2 + side
            value = product[:, side * width:(side + 1) * width]

            @pl.when(index == me)
            def _():
                arrived[me] = value

            @pl.when(index != me)
            def _():
                parts[index] = value
                part_copy(index).start()

        return carry

    lax.fori_loop(0, count // 2, one, 0)

    def take(step, carry):
        index = lax.rem(me + 1 + step, count)
        remote(parts.at[index], arrived.at[index], part_send.at[index],
               part_recv.at[index], owner_id(index)).wait_recv()
        return carry

    lax.fori_loop(0, count - 1, take, 0)
    bias = jnp.sum(arrived[...], axis=0).reshape(sharers, 2, local, width)
    chosen = samples_ref[:, pl.ds(pl.multiple_of(me * width, width), width)]
    chosen = chosen.reshape(sharers, local, width)
    pair = jnp.stack([bias[:, 1], chosen - bias[:, 0]], 1)
    coef_ref[me] = pair.reshape(sharers * 2 * local, width).astype(jnp.bfloat16)

    def spread(step, carry):
        index = lax.rem(me + 1 + step, count)
        remote(coef_ref.at[me], coef_ref.at[me], coef_send.at[index],
               coef_recv.at[me], owner_id(index)).start()
        return carry

    lax.fori_loop(0, count - 1, spread, 0)

    def finish(step, carry):
        index = lax.rem(me + 1 + step, count)
        part_copy(index).wait_send()
        remote(coef_ref.at[me], coef_ref.at[index], coef_send.at[index],
               coef_recv.at[index], owner_id(index)).wait()
        return carry

    lax.fori_loop(0, count - 1, finish, 0)
    for send in sends:
        send.wait_send()


def field_phase(count, sharers, coef_ref, columns_ref, vectors_ref, field_ref, whole_ref,
                 spread, blocks, total, full, outgoing, incoming, finished,
                 load_sem, column_send, column_recv, walk_send, walk_recv,
                 row_send, row_recv):
    me, walk = position(), lax.axis_index("walk")
    local = columns_ref.shape[0]
    row_block = columns_ref.shape[1]
    orbitals = vectors_ref.shape[2]
    chunks = vectors_ref.shape[0] // VECTORS
    groups = row_block // ROWS
    lines = coef_ref.shape[1]
    depth = VECTORS * HALF

    def load(step):
        return block_load(vectors_ref, blocks, load_sem, step)

    vector_at = lax.broadcasted_iota(jnp.int32, (LANES, depth), 0)
    place = lax.broadcasted_iota(jnp.int32, (LANES, depth), 1)
    row_at = lax.broadcasted_iota(jnp.int32, (HALF, depth), 0)
    row_place = lax.broadcasted_iota(jnp.int32, (HALF, depth), 1)
    diagonal = (lax.rem(row_place, HALF) == row_at).astype(jnp.float32)

    picks = (vector_at == place // HALF).astype(jnp.bfloat16)

    def widen(block):
        repeated = jnp.dot(coef_ref[block], picks, preferred_element_type=jnp.float32)
        wide = repeated[:, None, :] * diagonal[None]
        spread[block] = wide.reshape(lines * HALF, depth).astype(jnp.bfloat16)

    widen(0)

    def walk_copy(group, step, arriving):
        other = lax.rem(walk + step, sharers) if not arriving else lax.rem(
            walk + sharers - step, sharers)
        return remote(outgoing.at[group, other], incoming.at[group, other if arriving else walk],
                      walk_send.at[group, other], walk_recv.at[group, other if arriving else walk],
                      {"walk": other})

    def row_copy(group, index, arriving):
        giver = index if arriving else me
        at = pl.ds(pl.multiple_of(giver * row_block + group * ROWS, ROWS), ROWS)
        return remote(finished.at[group, index], field_ref.at[:, at, :],
                      row_send.at[group, index], row_recv.at[group, giver], owner_id(index))

    def deliver(group):
        result = full[group, walk]
        for step in range(1, sharers):
            walk_copy(group, step, True).wait_recv()
            other = lax.rem(walk + sharers - step, sharers)
            result = result + incoming[group, other].astype(jnp.float32)
        finished[group] = result.astype(jnp.bfloat16)

        def send_rows(step, carry):
            row_copy(group, lax.rem(me + 1 + step, count), False).start()
            return carry

        lax.fori_loop(0, count - 1, send_rows, 0)
        field_ref[:, pl.ds(pl.multiple_of(me * row_block + group * ROWS, ROWS), ROWS), :] = (
            finished[group, me]
        )

    for group in range(groups):
        total[...] = jnp.zeros_like(total)

        def add(chunk, carry):
            step = group * chunks + chunk

            @pl.when(step + DEPTH - 1 < groups * chunks)
            def _():
                load(step + DEPTH - 1).start()

            load(step).wait()
            slot = lax.rem(step, DEPTH)
            upper = blocks[slot, :, :HALF, :].reshape(depth, orbitals)
            lower = blocks[slot, :, HALF:, :].reshape(depth, orbitals)
            total[...] += jnp.dot(
                spread[chunk], jnp.concatenate([upper, lower], axis=1),
                preferred_element_type=jnp.float32,
            )
            if group == 0:
                widen(jnp.minimum(chunk + 1, chunks - 1))
            return carry

        lax.fori_loop(0, chunks, add, 0)
        result = total[...].reshape(sharers, 2, local, HALF, 2 * orbitals)
        result = jnp.concatenate([result[..., :orbitals], result[..., orbitals:]], axis=3)
        for part in range(2):
            full[group, :, :, part] = result[:, part]
            outgoing[group, :, :, part] = result[:, part].astype(jnp.bfloat16)
        for step in range(1, sharers):
            walk_copy(group, step, False).start()
        if group > 0:
            deliver(group - 1)
    deliver(groups - 1)

    def finish(step, carry):
        index = lax.rem(me + 1 + step, count)
        there = pl.ds(pl.multiple_of(index * row_block, ROWS), row_block)
        remote(columns_ref.at[index], whole_ref.at[there, :], column_send.at[index],
               column_recv.at[index], owner_id(index)).wait()
        for group in range(groups):
            row_copy(group, index, False).wait_send()
            row_copy(group, index, True).wait_recv()
        return carry

    lax.fori_loop(0, count - 1, finish, 0)
    for group in range(groups):
        for step in range(1, sharers):
            walk_copy(group, step, False).wait_send()


def two_parts(value):
    high = value.astype(jnp.bfloat16)
    return high, (value - high.astype(jnp.float32)).astype(jnp.bfloat16)


def exact(left, right, axis=1):
    left_high, left_low = two_parts(left)
    right_high, right_low = two_parts(right)
    return lax.dot_general(
        jnp.concatenate([left_high, left_low, left_high], axis=axis),
        jnp.concatenate([right_high, right_high, right_low], axis=0),
        (((axis,), (0,)), ((), ())), preferred_element_type=jnp.float32,
    )


def walker_phase(count, sharers, electrons, field_ref, whole_ref, source_ref, out_ref,
                 moved, grid, send_sem, recv_sem, rows):
    me, walk = position(), lax.axis_index("walk")
    row_block = rows.shape[1]
    orbitals = field_ref.shape[1]
    others = partners(count, sharers)

    def swap(value, sign):
        return jnp.concatenate([-sign * value[:, LANES:], sign * value[:, :LANES]], axis=1)

    current = whole_ref[...].astype(jnp.float32)
    summed = current
    for order_index in range(1, TERMS + 1):
        rounded = current.astype(jnp.bfloat16)
        real = jnp.dot(field_ref[0], rounded, preferred_element_type=jnp.float32)
        imag = jnp.dot(field_ref[1], rounded, preferred_element_type=jnp.float32)
        current = (real + swap(imag, 1.0)) / order_index
        summed = summed + current
    squares = exact(summed, summed, 0) / orbitals
    gram_real = squares[:LANES, :LANES] + squares[LANES:, LANES:]
    gram_imag = squares[:LANES, LANES:] - squares[LANES:, :LANES]
    size = 2 * LANES
    identity = (
        lax.broadcasted_iota(jnp.int32, (size, size), 0)
        == lax.broadcasted_iota(jnp.int32, (size, size), 1)
    ).astype(jnp.float32)
    scale = jnp.sum(gram_real * identity[:LANES, :LANES]) / electrons
    top = jnp.concatenate([gram_real, gram_imag], axis=1)
    bottom = jnp.concatenate([-gram_imag, gram_real], axis=1)
    iterate = jnp.concatenate([top, bottom], axis=0) / scale
    step_of = 1.5 * identity - 0.5 * iterate
    root = step_of
    for sweep_index in range(1, NS_STEPS):
        iterate = exact(iterate, step_of)
        step_of = 1.5 * identity - 0.5 * exact(root, iterate)
        root = exact(step_of, root)
    normalized = exact(summed, root * lax.rsqrt(scale))
    rows[...] = normalized.reshape(count, row_block, size).astype(jnp.bfloat16)

    mine = walk * count + me
    for across, step, target in others:
        index = lax.rem(me + step, count)
        remote(rows.at[index], moved.at[mine], send_sem.at[across, step],
               recv_sem.at[across, step], target).start()
    moved[mine] = rows[me]
    for across, step, target in others:
        index = lax.rem(me + step, count)
        giver = lax.rem(walk + sharers - across, sharers) * count + lax.rem(
            me + count - step, count)
        remote(rows.at[index], moved.at[giver], send_sem.at[across, step],
               recv_sem.at[across, step], target).wait()
    for walker in range(count):
        taken = moved[source_ref[walker]].astype(jnp.float32)
        for side in range(2):
            grid[:, 2 * walker + side, :] = taken[:, side * LANES:(side + 1) * LANES]
    for start, value in to_flat(grid, electrons):
        out_ref[:, start:start + LANES] = value


def step_kernel(count, sharers, electrons, walkers_ref, inverse_ref, half_ref, samples_ref, source_ref,
                vectors_ref, out_ref, moved, columns, matrices, rows_in, grid, half, theta, parts, arrived, coef, field, whole, spread,
                blocks, total, full, outgoing, incoming, finished, rows, half_sem, block_sem,
                theta_send, theta_recv, part_send, part_recv, coef_send, coef_recv,
                column_send, column_recv, walk_send, walk_recv, row_send, row_recv,
                out_send, out_recv):
    me = position()

    def first_half(step, carry):
        half_load(half_ref, half, half_sem, lax.rem((me // 2) * 2 + 2 + step, count)).start()
        return carry

    lax.fori_loop(0, count, first_half, 0)

    def first_blocks(step, carry):
        block_load(vectors_ref, blocks, block_sem, step).start()
        return carry

    lax.fori_loop(0, DEPTH - 1, first_blocks, 0)
    others = [target for _, _, target in partners(count, sharers)]
    barrier = greet(others)
    theta_phase(walkers_ref, inverse_ref, theta, columns, matrices, rows_in, grid)
    pl.semaphore_wait(barrier, len(others))
    bias_phase(count, sharers, half_ref, samples_ref, coef, half, theta, parts,
               arrived, half_sem, theta_send, theta_recv, part_send, part_recv, coef_send,
               coef_recv)
    column_phase(count, columns, whole, column_send, column_recv)
    field_phase(count, sharers, coef, columns, vectors_ref, field, whole, spread, blocks,
                total, full, outgoing, incoming, finished, block_sem, column_send, column_recv,
                walk_send, walk_recv, row_send, row_recv)
    walker_phase(count, sharers, electrons, field, whole, source_ref, out_ref, moved, grid,
                 out_send, out_recv, rows)


def body(walkers, correlation_inverse, half_vectors, field_vectors, samples, source):
    local_walkers = walkers.shape[0]
    vectors, row_block, orbitals = field_vectors.shape
    electrons = correlation_inverse.shape[2]
    flat = row_block * electrons
    count = lax.axis_size(("chol", "orb"))
    sharers = lax.axis_size("walk")
    width = vectors // count
    fits = (
        count == local_walkers and row_block % ROWS == 0 and local_walkers % HALF == 0
        and width % LANES == 0 and width == LANES == VECTORS
        and electrons <= LANES and orbitals % LANES == 0
        and flat % LANES == 0 and count % 2 == 0 and electrons % ROWS == 0
        and (row_block // ROWS) * (vectors // VECTORS) >= DEPTH
    )
    if not fits:
        return plain_body(
            walkers, correlation_inverse, half_vectors, field_vectors, samples, source
        )
    lines = sharers * 2 * local_walkers
    groups = row_block // ROWS
    chunks = vectors // VECTORS
    vmem, anywhere = pltpu.VMEM, pl.ANY
    dma = pltpu.SemaphoreType.DMA
    half_type, full_type = jnp.bfloat16, jnp.float32
    result = pl.pallas_call(
        functools.partial(step_kernel, count, sharers, electrons),
        out_shape=jax.ShapeDtypeStruct((2 * local_walkers, flat), walkers.dtype),
        in_specs=[
            pl.BlockSpec(memory_space=place) for place in (vmem, vmem, anywhere, vmem, pltpu.SMEM, anywhere)
        ],
        out_specs=pl.BlockSpec(memory_space=vmem),
        scratch_shapes=[
            vmem((sharers * local_walkers, row_block, 2 * LANES), half_type),
            vmem((local_walkers, row_block, 2 * LANES), half_type),
            vmem((2, 6 * LANES, 2 * LANES), half_type),
            vmem((row_block, 2 * local_walkers, LANES), full_type),
            vmem((row_block, 2 * local_walkers, LANES), full_type),
            vmem((count, width, flat), half_type),
            vmem((sharers, 2 * local_walkers, flat), half_type),
            vmem((count, lines, width), full_type),
            vmem((count, lines, width), full_type),
            vmem((count, lines, width), half_type),
            vmem((2, orbitals, orbitals), half_type),
            vmem((orbitals, 2 * LANES), half_type),
            vmem((chunks, lines * HALF, VECTORS * HALF), half_type),
            vmem((DEPTH, VECTORS, ROWS, orbitals), half_type),
            vmem((lines * HALF, 2 * orbitals), full_type),
            vmem((groups, sharers, local_walkers, 2, ROWS, orbitals), full_type),
            vmem((groups, sharers, local_walkers, 2, ROWS, orbitals), half_type),
            vmem((groups, sharers, local_walkers, 2, ROWS, orbitals), half_type),
            vmem((groups, local_walkers, 2, ROWS, orbitals), half_type),
            vmem((count, row_block, 2 * LANES), half_type),
            dma((count,)), dma((DEPTH,)),
            dma((sharers,)), dma((sharers,)),
            dma((count,)), dma((count,)), dma((count,)), dma((count,)),
            dma((count,)), dma((count,)),
            dma((groups, sharers)), dma((groups, sharers)),
            dma((groups, count)), dma((groups, count)),
            dma((sharers, count)), dma((sharers, count)),
        ],
        compiler_params=pltpu.CompilerParams(
            collective_id=0, has_side_effects=True, vmem_limit_bytes=VMEM_LIMIT
        ),
    )(walkers.reshape(2 * local_walkers, flat), correlation_inverse, half_vectors, samples, source,
      field_vectors)
    return result.reshape(walkers.shape)


def solution(mesh):
    placed = (
        P(("groups", "walk"), None, ("chol", "orb")),
        P(("groups", "walk"), None, None, None),
        P(("groups", "walk"), ("chol", "orb")),
        P(("groups", "walk"), ("chol", "orb"), None),
        P("groups", "walk"),
        P(("groups", "walk")),
    )
    return jax.shard_map(
        body,
        mesh=mesh,
        in_specs=placed,
        out_specs=P(("groups", "walk"), None, ("chol", "orb")),
        check_vma=False,
    )
```

```python
import functools

import jax
import jax.numpy as jnp
from jax import lax
from jax.experimental import pallas as pl
from jax.experimental.pallas import tpu as pltpu
from jax.sharding import PartitionSpec as P

TERMS = 4
NS_STEPS = 2


def for_sending(shard):
    return jax.tree.map(lambda a: a.astype(jnp.bfloat16) if a.dtype == jnp.float32 else a, shard)


def complex_product(left_real, left_imag, right_real, right_imag, formula):
    first = jnp.einsum(formula, left_real, right_real, precision=lax.Precision.HIGHEST)
    second = jnp.einsum(formula, left_imag, right_imag, precision=lax.Precision.HIGHEST)
    third = jnp.einsum(formula, left_real, right_imag, precision=lax.Precision.HIGHEST)
    fourth = jnp.einsum(formula, left_imag, right_real, precision=lax.Precision.HIGHEST)
    return (first - second, third + fourth)


def normalizer(gram_real, gram_imag):
    electrons = gram_real.shape[-1]
    identity = jnp.eye(electrons, dtype=jnp.float32)
    scale_factor = jnp.trace(gram_real, axis1=1, axis2=2) / electrons
    iter_real = gram_real / scale_factor[:, None, None]
    iter_imag = gram_imag / scale_factor[:, None, None]
    root_real = jnp.broadcast_to(identity, gram_real.shape)
    root_imag = jnp.zeros_like(gram_real)
    for sweep_index in range(NS_STEPS):
        prod_real, prod_imag = complex_product(
            root_real, root_imag, iter_real, iter_imag, "wij,wjk->wik"
        )
        step_real = 1.5 * identity - 0.5 * prod_real
        step_imag = -0.5 * prod_imag
        iter_real, iter_imag = complex_product(
            iter_real, iter_imag, step_real, step_imag, "wij,wjk->wik"
        )
        root_real, root_imag = complex_product(
            step_real, step_imag, root_real, root_imag, "wij,wjk->wik"
        )
    inverse_root = lax.rsqrt(scale_factor)[:, None, None]
    return (root_real * inverse_root, root_imag * inverse_root)


def field_apply(field_block, values):
    next_real = jnp.einsum(
        "wab,wbn->wan", field_block[:, 0], values[:, 0], preferred_element_type=jnp.float32
    )
    next_real = next_real - jnp.einsum(
        "wab,wbn->wan", field_block[:, 1], values[:, 1], preferred_element_type=jnp.float32
    )
    next_imag = jnp.einsum(
        "wab,wbn->wan", field_block[:, 0], values[:, 1], preferred_element_type=jnp.float32
    )
    next_imag = next_imag + jnp.einsum(
        "wab,wbn->wan", field_block[:, 1], values[:, 0], preferred_element_type=jnp.float32
    )
    return jnp.stack([next_real, next_imag], 1)


def plain_body(walkers, correlation_inverse, half_vectors, field_vectors, samples, source):
    local_walkers = walkers.shape[0]
    row_block = field_vectors.shape[1]
    orbitals = field_vectors.shape[2]
    electrons = correlation_inverse.shape[2]
    grid = walkers.reshape(local_walkers, 2, row_block, electrons)
    theta_real, theta_imag = complex_product(
        grid[:, 0], grid[:, 1], correlation_inverse[:, 0], correlation_inverse[:, 1], "wmk,wkn->wmn"
    )
    theta = (
        jnp.stack([theta_real, theta_imag], 1)
        .reshape(local_walkers, 2, row_block * electrons)
        .astype(jnp.bfloat16)
    )
    all_theta = lax.all_gather(theta, "walk", axis=0, tiled=True)
    bias_part = jnp.einsum(
        "wcj,gj->wcg", all_theta, half_vectors, preferred_element_type=jnp.float32
    )
    bias = lax.psum(bias_part, ("chol", "orb"))
    coefficient = jnp.stack([bias[:, 1], samples - bias[:, 0]], 1).astype(jnp.bfloat16)
    field_part = jnp.einsum(
        "wcg,gab->wcab", coefficient, field_vectors, preferred_element_type=jnp.float32
    )
    field = lax.psum_scatter(field_part, "walk", scatter_dimension=0, tiled=True).astype(
        jnp.bfloat16
    )
    devices_rows = lax.axis_size(("chol", "orb"))
    sharers = devices_rows // local_walkers
    col_width = electrons // sharers
    parted = grid.reshape(local_walkers, 2, row_block, sharers, col_width)
    parted = parted.transpose(0, 3, 1, 2, 4).reshape(devices_rows, 2, row_block, col_width)
    columns = lax.all_to_all(
        parted.astype(jnp.bfloat16), ("chol", "orb"), split_axis=0, concat_axis=2, tiled=True
    ).astype(parted.dtype)
    spread = jnp.broadcast_to(field[:, None], (local_walkers, sharers, 2, row_block, orbitals))
    spread = spread.reshape(devices_rows, 2, row_block, orbitals)
    whole_field = lax.all_to_all(spread, ("chol", "orb"), split_axis=0, concat_axis=2, tiled=True)
    current = columns
    col_summed = columns
    for order_index in range(1, TERMS + 1):
        current = field_apply(whole_field, current.astype(jnp.bfloat16)) / order_index
        col_summed = col_summed + current
    returned = lax.all_to_all(
        col_summed.astype(jnp.bfloat16), ("chol", "orb"), split_axis=2, concat_axis=0, tiled=True
    ).astype(col_summed.dtype)
    returned = returned.reshape(local_walkers, sharers, 2, row_block, col_width)
    summed = returned.transpose(0, 2, 3, 1, 4).reshape(local_walkers, 2, row_block, electrons)
    whole = lax.all_gather(summed.astype(jnp.bfloat16), ("chol", "orb"), axis=2, tiled=True).astype(
        summed.dtype
    )
    gram_real, gram_imag = complex_product(
        whole[:, 0], -whole[:, 1], whole[:, 0], whole[:, 1], "wmi,wmj->wij"
    )
    gram_real = gram_real / orbitals
    gram_imag = gram_imag / orbitals
    root_real, root_imag = normalizer(gram_real, gram_imag)
    norm_real, norm_imag = complex_product(
        summed[:, 0], summed[:, 1], root_real, root_imag, "wmk,wkn->wmn"
    )
    normalized = jnp.stack([norm_real, norm_imag], 1).reshape(
        local_walkers, 2, row_block * electrons
    )
    moved = lax.all_gather(for_sending(normalized), "walk", axis=0, tiled=True).astype(
        normalized.dtype
    )
    return jnp.take(moved, source, axis=0)


MESH = pl.DeviceIdType.MESH
LANES = 128
HALF = 8
ROWS = 16
VECTORS = 128
DEPTH = 16
VMEM_LIMIT = 60 * 1024 * 1024


def owner_id(index):
    orbs = lax.axis_size("orb")
    return {"chol": index // orbs, "orb": lax.rem(index, orbs)}


def position():
    return lax.axis_index("chol") * lax.axis_size("orb") + lax.axis_index("orb")


def greet(devices):
    barrier = pltpu.get_barrier_semaphore()
    for device in devices:
        pl.semaphore_signal(barrier, inc=1, device_id=device, device_id_type=MESH)
    return barrier


def partners(count, sharers):
    me, walk = position(), lax.axis_index("walk")
    others = []
    for across in range(sharers):
        for step in range(count):
            if across + step > 0:
                target = owner_id(lax.rem(me + step, count))
                target["walk"] = lax.rem(walk + across, sharers)
                others.append((across, step, target))
    return others


def remote(source, target, send, recv, device):
    return pltpu.make_async_remote_copy(
        src_ref=source, dst_ref=target, send_sem=send, recv_sem=recv,
        device_id=device, device_id_type=MESH,
    )


def to_rows(flat_ref, grid, electrons):
    lane = lax.broadcasted_iota(jnp.int32, (grid.shape[1], LANES), 1)

    def tile_at(start):
        return flat_ref[:, :, start:start + LANES].reshape(grid.shape[1], LANES)

    for row in range(grid.shape[0]):
        start, shift = row * electrons // LANES * LANES, row * electrons % LANES
        back = (LANES - shift) % LANES
        value = pltpu.roll(tile_at(start), back, 1)
        if shift + electrons > LANES:
            after = pltpu.roll(tile_at(start + LANES), back, 1)
            value = jnp.where(lane < LANES - shift, value, after)
        grid[row] = jnp.where(lane < electrons, value, 0.0)


def to_flat(grid, electrons):
    lane = lax.broadcasted_iota(jnp.int32, (grid.shape[1], LANES), 1)
    for tile in range(grid.shape[0] * electrons // LANES):
        start = tile * LANES
        value = None
        for row in range(start // electrons, (start + LANES - 1) // electrons + 1):
            moved = pltpu.roll(grid[row], row * electrons % LANES, 1)
            value = moved if value is None else jnp.where(
                lane < row * electrons - start, value, moved)
        yield start, value


def theta_phase(walkers_ref, inverse_ref, theta, columns, matrices, rows_in, grid):
    walk = lax.axis_index("walk")
    local = inverse_ref.shape[0]
    electrons = inverse_ref.shape[2]
    to_rows(walkers_ref, rows_in, electrons)
    size = 2 * LANES
    matrices[...] = jnp.zeros_like(matrices)
    for walker in range(local):
        matrix = matrices.at[walker % 2]
        real_parts = two_parts(inverse_ref[walker, 0])
        imag_parts = two_parts(inverse_ref[walker, 1])
        for place, part in enumerate((0, 0, 1)):
            first, second = place * size, place * size + LANES
            matrix[first:first + electrons, :electrons] = real_parts[part]
            matrix[first:first + electrons, LANES:LANES + electrons] = imag_parts[part]
            matrix[second:second + electrons, :electrons] = -imag_parts[part]
            matrix[second:second + electrons, LANES:LANES + electrons] = real_parts[part]
        pair = [rows_in[:, 2 * walker + side, :] for side in range(2)]
        high, low = two_parts(jnp.concatenate(pair, axis=1))
        columns[walker] = high
        rotated = jnp.dot(jnp.concatenate([high, low, high], axis=1), matrix[...],
                          preferred_element_type=jnp.float32)
        grid[:, walker, :] = rotated[:, :LANES]
        grid[:, local + walker, :] = rotated[:, LANES:]
    for start, value in to_flat(grid, electrons):
        theta[walk, :, start:start + LANES] = value.astype(jnp.bfloat16)


def half_load(half_ref, half, load_sem, index):
    width = half.shape[1]
    return pltpu.make_async_copy(
        half_ref.at[pl.ds(pl.multiple_of(index * width, width), width), :],
        half.at[index], load_sem.at[index],
    )


def block_load(vectors_ref, blocks, load_sem, step):
    chunks = vectors_ref.shape[0] // VECTORS
    group, chunk = step // chunks, lax.rem(step, chunks)
    slot = lax.rem(step, DEPTH)
    return pltpu.make_async_copy(
        vectors_ref.at[pl.ds(pl.multiple_of(chunk * VECTORS, VECTORS), VECTORS),
                       pl.ds(pl.multiple_of(group * ROWS, ROWS), ROWS), :],
        blocks.at[slot], load_sem.at[slot],
    )


def column_phase(count, columns_ref, whole_ref, column_send, column_recv):
    me = position()
    row_block = columns_ref.shape[1]
    here = pl.ds(pl.multiple_of(me * row_block, ROWS), row_block)

    def send_columns(step, carry):
        index = lax.rem(me + 1 + step, count)
        remote(columns_ref.at[index], whole_ref.at[here, :], column_send.at[index],
               column_recv.at[me], owner_id(index)).start()
        return carry

    lax.fori_loop(0, count - 1, send_columns, 0)
    whole_ref[here, :] = columns_ref[me]


def bias_phase(count, sharers, half_ref, samples_ref, coef_ref,
                half, theta, parts, arrived, load_sem, theta_send, theta_recv,
                part_send, part_recv, coef_send, coef_recv):
    me, walk = position(), lax.axis_index("walk")
    width = half.shape[1]
    local = theta.shape[1] // 2

    def load(index):
        return half_load(half_ref, half, load_sem, index)

    sends = []
    for step in range(1, sharers):
        other = lax.rem(walk + step, sharers)
        sends.append(remote(theta.at[walk], theta.at[walk], theta_send.at[step],
                            theta_recv.at[walk], {"walk": other}))
        sends[-1].start()
    for step in range(1, sharers):
        other = lax.rem(walk + step, sharers)
        remote(theta.at[walk], theta.at[other], theta_send.at[step],
               theta_recv.at[other], {"walk": other}).wait_recv()

    def part_copy(index):
        return remote(parts.at[index], arrived.at[me], part_send.at[index],
                      part_recv.at[me], owner_id(index))

    def one(step, carry):
        pair = lax.rem(me // 2 + 1 + step, count // 2)
        for side in range(2):
            load(pair * 2 + side).wait()
        product = lax.dot_general(
            theta[...].reshape(sharers * 2 * local, theta.shape[2]),
            half[pl.ds(pair * 2, 2)].reshape(2 * width, theta.shape[2]),
            (((1,), (1,)), ((), ())), preferred_element_type=jnp.float32,
        )
        for side in range(2):
            index = pair * 2 + side
            value = product[:, side * width:(side + 1) * width]

            @pl.when(index == me)
            def _():
                arrived[me] = value

            @pl.when(index != me)
            def _():
                parts[index] = value
                part_copy(index).start()

        return carry

    lax.fori_loop(0, count // 2, one, 0)

    def take(step, carry):
        index = lax.rem(me + 1 + step, count)
        remote(parts.at[index], arrived.at[index], part_send.at[index],
               part_recv.at[index], owner_id(index)).wait_recv()
        return carry

    lax.fori_loop(0, count - 1, take, 0)
    bias = jnp.sum(arrived[...], axis=0).reshape(sharers, 2, local, width)
    chosen = samples_ref[:, pl.ds(pl.multiple_of(me * width, width), width)]
    chosen = chosen.reshape(sharers, local, width)
    pair = jnp.stack([bias[:, 1], chosen - bias[:, 0]], 1)
    coef_ref[me] = pair.reshape(sharers * 2 * local, width).astype(jnp.bfloat16)

    def spread(step, carry):
        index = lax.rem(me + 1 + step, count)
        remote(coef_ref.at[me], coef_ref.at[me], coef_send.at[index],
               coef_recv.at[me], owner_id(index)).start()
        return carry

    lax.fori_loop(0, count - 1, spread, 0)

    def finish(step, carry):
        index = lax.rem(me + 1 + step, count)
        part_copy(index).wait_send()
        remote(coef_ref.at[me], coef_ref.at[index], coef_send.at[index],
               coef_recv.at[index], owner_id(index)).wait()
        return carry

    lax.fori_loop(0, count - 1, finish, 0)
    for send in sends:
        send.wait_send()


def field_phase(count, sharers, coef_ref, columns_ref, vectors_ref, field_ref, whole_ref,
                 spread, blocks, total, full, outgoing, incoming, finished,
                 load_sem, column_send, column_recv, walk_send, walk_recv,
                 row_send, row_recv):
    me, walk = position(), lax.axis_index("walk")
    local = columns_ref.shape[0]
    row_block = columns_ref.shape[1]
    orbitals = vectors_ref.shape[2]
    chunks = vectors_ref.shape[0] // VECTORS
    groups = row_block // ROWS
    lines = coef_ref.shape[1]
    depth = VECTORS * HALF

    def load(step):
        return block_load(vectors_ref, blocks, load_sem, step)

    vector_at = lax.broadcasted_iota(jnp.int32, (LANES, depth), 0)
    place = lax.broadcasted_iota(jnp.int32, (LANES, depth), 1)
    row_at = lax.broadcasted_iota(jnp.int32, (HALF, depth), 0)
    row_place = lax.broadcasted_iota(jnp.int32, (HALF, depth), 1)
    diagonal = (lax.rem(row_place, HALF) == row_at).astype(jnp.float32)

    picks = (vector_at == place // HALF).astype(jnp.bfloat16)

    def widen(block):
        repeated = jnp.dot(coef_ref[block], picks, preferred_element_type=jnp.float32)
        wide = repeated[:, None, :] * diagonal[None]
        spread[block] = wide.reshape(lines * HALF, depth).astype(jnp.bfloat16)

    widen(0)

    def walk_copy(group, step, arriving):
        other = lax.rem(walk + step, sharers) if not arriving else lax.rem(
            walk + sharers - step, sharers)
        return remote(outgoing.at[group, other], incoming.at[group, other if arriving else walk],
                      walk_send.at[group, other], walk_recv.at[group, other if arriving else walk],
                      {"walk": other})

    def row_copy(group, index, arriving):
        giver = index if arriving else me
        at = pl.ds(pl.multiple_of(giver * row_block + group * ROWS, ROWS), ROWS)
        return remote(finished.at[group, index], field_ref.at[:, at, :],
                      row_send.at[group, index], row_recv.at[group, giver], owner_id(index))

    def deliver(group):
        result = full[group, walk]
        for step in range(1, sharers):
            walk_copy(group, step, True).wait_recv()
            other = lax.rem(walk + sharers - step, sharers)
            result = result + incoming[group, other].astype(jnp.float32)
        finished[group] = result.astype(jnp.bfloat16)

        def send_rows(step, carry):
            row_copy(group, lax.rem(me + 1 + step, count), False).start()
            return carry

        lax.fori_loop(0, count - 1, send_rows, 0)
        field_ref[:, pl.ds(pl.multiple_of(me * row_block + group * ROWS, ROWS), ROWS), :] = (
            finished[group, me]
        )

    for group in range(groups):
        total[...] = jnp.zeros_like(total)

        def add(chunk, carry):
            step = group * chunks + chunk

            @pl.when(step + DEPTH - 1 < groups * chunks)
            def _():
                load(step + DEPTH - 1).start()

            load(step).wait()
            slot = lax.rem(step, DEPTH)
            upper = blocks[slot, :, :HALF, :].reshape(depth, orbitals)
            lower = blocks[slot, :, HALF:, :].reshape(depth, orbitals)
            total[...] += jnp.dot(
                spread[chunk], jnp.concatenate([upper, lower], axis=1),
                preferred_element_type=jnp.float32,
            )
            if group == 0:
                widen(jnp.minimum(chunk + 1, chunks - 1))
            return carry

        lax.fori_loop(0, chunks, add, 0)
        result = total[...].reshape(sharers, 2, local, HALF, 2 * orbitals)
        result = jnp.concatenate([result[..., :orbitals], result[..., orbitals:]], axis=3)
        for part in range(2):
            full[group, :, :, part] = result[:, part]
            outgoing[group, :, :, part] = result[:, part].astype(jnp.bfloat16)
        for step in range(1, sharers):
            walk_copy(group, step, False).start()
        if group > 0:
            deliver(group - 1)
    deliver(groups - 1)

    def finish(step, carry):
        index = lax.rem(me + 1 + step, count)
        there = pl.ds(pl.multiple_of(index * row_block, ROWS), row_block)
        remote(columns_ref.at[index], whole_ref.at[there, :], column_send.at[index],
               column_recv.at[index], owner_id(index)).wait()
        for group in range(groups):
            row_copy(group, index, False).wait_send()
            row_copy(group, index, True).wait_recv()
        return carry

    lax.fori_loop(0, count - 1, finish, 0)
    for group in range(groups):
        for step in range(1, sharers):
            walk_copy(group, step, False).wait_send()


def two_parts(value):
    high = value.astype(jnp.bfloat16)
    return high, (value - high.astype(jnp.float32)).astype(jnp.bfloat16)


def exact(left, right, axis=1):
    left_high, left_low = two_parts(left)
    right_high, right_low = two_parts(right)
    return lax.dot_general(
        jnp.concatenate([left_high, left_low, left_high], axis=axis),
        jnp.concatenate([right_high, right_high, right_low], axis=0),
        (((axis,), (0,)), ((), ())), preferred_element_type=jnp.float32,
    )


def walker_phase(count, sharers, electrons, field_ref, whole_ref, source_ref, out_ref,
                 moved, grid, send_sem, recv_sem, rows):
    me, walk = position(), lax.axis_index("walk")
    row_block = rows.shape[1]
    orbitals = field_ref.shape[1]
    others = partners(count, sharers)

    def swap(value, sign):
        return jnp.concatenate([-sign * value[:, LANES:], sign * value[:, :LANES]], axis=1)

    current = whole_ref[...].astype(jnp.float32)
    summed = current
    for order_index in range(1, TERMS + 1):
        rounded = current.astype(jnp.bfloat16)
        real = jnp.dot(field_ref[0], rounded, preferred_element_type=jnp.float32)
        imag = jnp.dot(field_ref[1], rounded, preferred_element_type=jnp.float32)
        current = (real + swap(imag, 1.0)) / order_index
        summed = summed + current
    squares = exact(summed, summed, 0) / orbitals
    gram_real = squares[:LANES, :LANES] + squares[LANES:, LANES:]
    gram_imag = squares[:LANES, LANES:] - squares[LANES:, :LANES]
    size = 2 * LANES
    identity = (
        lax.broadcasted_iota(jnp.int32, (size, size), 0)
        == lax.broadcasted_iota(jnp.int32, (size, size), 1)
    ).astype(jnp.float32)
    scale = jnp.sum(gram_real * identity[:LANES, :LANES]) / electrons
    top = jnp.concatenate([gram_real, gram_imag], axis=1)
    bottom = jnp.concatenate([-gram_imag, gram_real], axis=1)
    iterate = jnp.concatenate([top, bottom], axis=0) / scale
    step_of = 1.5 * identity - 0.5 * iterate
    root = step_of
    for sweep_index in range(1, NS_STEPS):
        iterate = exact(iterate, step_of)
        step_of = 1.5 * identity - 0.5 * exact(root, iterate)
        root = exact(step_of, root)
    normalized = exact(summed, root * lax.rsqrt(scale))
    rows[...] = normalized.reshape(count, row_block, size).astype(jnp.bfloat16)

    mine = walk * count + me
    for across, step, target in others:
        index = lax.rem(me + step, count)
        remote(rows.at[index], moved.at[mine], send_sem.at[across, step],
               recv_sem.at[across, step], target).start()
    moved[mine] = rows[me]
    for across, step, target in others:
        index = lax.rem(me + step, count)
        giver = lax.rem(walk + sharers - across, sharers) * count + lax.rem(
            me + count - step, count)
        remote(rows.at[index], moved.at[giver], send_sem.at[across, step],
               recv_sem.at[across, step], target).wait()
    for walker in range(count):
        taken = moved[source_ref[walker]].astype(jnp.float32)
        for side in range(2):
            grid[:, 2 * walker + side, :] = taken[:, side * LANES:(side + 1) * LANES]
    for start, value in to_flat(grid, electrons):
        out_ref[:, :, start:start + LANES] = value.reshape(count, 2, LANES)


def step_kernel(count, sharers, electrons, walkers_ref, inverse_ref, half_ref, samples_ref, source_ref,
                vectors_ref, out_ref, moved, columns, matrices, rows_in, grid, half, theta, parts, arrived, coef, field, whole, spread,
                blocks, total, full, outgoing, incoming, finished, rows, half_sem, block_sem,
                theta_send, theta_recv, part_send, part_recv, coef_send, coef_recv,
                column_send, column_recv, walk_send, walk_recv, row_send, row_recv,
                out_send, out_recv):
    me = position()

    def first_half(step, carry):
        half_load(half_ref, half, half_sem, lax.rem((me // 2) * 2 + 2 + step, count)).start()
        return carry

    lax.fori_loop(0, count, first_half, 0)

    def first_blocks(step, carry):
        block_load(vectors_ref, blocks, block_sem, step).start()
        return carry

    lax.fori_loop(0, DEPTH - 1, first_blocks, 0)
    others = [target for _, _, target in partners(count, sharers)]
    barrier = greet(others)
    theta_phase(walkers_ref, inverse_ref, theta, columns, matrices, rows_in, grid)
    pl.semaphore_wait(barrier, len(others))
    bias_phase(count, sharers, half_ref, samples_ref, coef, half, theta, parts,
               arrived, half_sem, theta_send, theta_recv, part_send, part_recv, coef_send,
               coef_recv)
    column_phase(count, columns, whole, column_send, column_recv)
    field_phase(count, sharers, coef, columns, vectors_ref, field, whole, spread, blocks,
                total, full, outgoing, incoming, finished, block_sem, column_send, column_recv,
                walk_send, walk_recv, row_send, row_recv)
    walker_phase(count, sharers, electrons, field, whole, source_ref, out_ref, moved, grid,
                 out_send, out_recv, rows)


def body(walkers, correlation_inverse, half_vectors, field_vectors, samples, source):
    local_walkers = walkers.shape[0]
    vectors, row_block, orbitals = field_vectors.shape
    electrons = correlation_inverse.shape[2]
    flat = row_block * electrons
    count = lax.axis_size(("chol", "orb"))
    sharers = lax.axis_size("walk")
    width = vectors // count
    fits = (
        count == local_walkers and row_block % ROWS == 0 and local_walkers % HALF == 0
        and width % LANES == 0 and width == LANES == VECTORS
        and electrons <= LANES and orbitals % LANES == 0
        and flat % LANES == 0 and count % 2 == 0 and electrons % ROWS == 0
        and (row_block // ROWS) * (vectors // VECTORS) >= DEPTH
    )
    if not fits:
        return plain_body(
            walkers, correlation_inverse, half_vectors, field_vectors, samples, source
        )
    lines = sharers * 2 * local_walkers
    groups = row_block // ROWS
    chunks = vectors // VECTORS
    vmem, anywhere = pltpu.VMEM, pl.ANY
    dma = pltpu.SemaphoreType.DMA
    half_type, full_type = jnp.bfloat16, jnp.float32
    result = pl.pallas_call(
        functools.partial(step_kernel, count, sharers, electrons),
        out_shape=jax.ShapeDtypeStruct(walkers.shape, walkers.dtype),
        in_specs=[
            pl.BlockSpec(memory_space=place) for place in (vmem, vmem, anywhere, vmem, pltpu.SMEM, anywhere)
        ],
        out_specs=pl.BlockSpec(memory_space=vmem),
        scratch_shapes=[
            vmem((sharers * local_walkers, row_block, 2 * LANES), half_type),
            vmem((local_walkers, row_block, 2 * LANES), half_type),
            vmem((2, 6 * LANES, 2 * LANES), half_type),
            vmem((row_block, 2 * local_walkers, LANES), full_type),
            vmem((row_block, 2 * local_walkers, LANES), full_type),
            vmem((count, width, flat), half_type),
            vmem((sharers, 2 * local_walkers, flat), half_type),
            vmem((count, lines, width), full_type),
            vmem((count, lines, width), full_type),
            vmem((count, lines, width), half_type),
            vmem((2, orbitals, orbitals), half_type),
            vmem((orbitals, 2 * LANES), half_type),
            vmem((chunks, lines * HALF, VECTORS * HALF), half_type),
            vmem((DEPTH, VECTORS, ROWS, orbitals), half_type),
            vmem((lines * HALF, 2 * orbitals), full_type),
            vmem((groups, sharers, local_walkers, 2, ROWS, orbitals), full_type),
            vmem((groups, sharers, local_walkers, 2, ROWS, orbitals), half_type),
            vmem((groups, sharers, local_walkers, 2, ROWS, orbitals), half_type),
            vmem((groups, local_walkers, 2, ROWS, orbitals), half_type),
            vmem((count, row_block, 2 * LANES), half_type),
            dma((count,)), dma((DEPTH,)),
            dma((sharers,)), dma((sharers,)),
            dma((count,)), dma((count,)), dma((count,)), dma((count,)),
            dma((count,)), dma((count,)),
            dma((groups, sharers)), dma((groups, sharers)),
            dma((groups, count)), dma((groups, count)),
            dma((sharers, count)), dma((sharers, count)),
        ],
        compiler_params=pltpu.CompilerParams(
            collective_id=0, has_side_effects=True, vmem_limit_bytes=VMEM_LIMIT
        ),
    )(walkers, correlation_inverse, half_vectors, samples, source,
      field_vectors)
    return result


def solution(mesh):
    placed = (
        P(("groups", "walk"), None, ("chol", "orb")),
        P(("groups", "walk"), None, None, None),
        P(("groups", "walk"), ("chol", "orb")),
        P(("groups", "walk"), ("chol", "orb"), None),
        P("groups", "walk"),
        P(("groups", "walk")),
    )
    return jax.shard_map(
        body,
        mesh=mesh,
        in_specs=placed,
        out_specs=P(("groups", "walk"), None, ("chol", "orb")),
        check_vma=False,
    )
```
